256 devices in a mesh: row: 32 (over y, z_hi, core), col: 8 (over z_lo, x).
Axes of the slice: x: 4, y: 4, z: 8 (z_hi: 4, z_lo: 2; z = z_hi * 2 + z_lo), core: 2. Of those that a mesh axis runs over, the one named last changes fastest.
Arguments:
- grad_out: bfloat16 [4096, 16384], P('col', 'row'), may hold values from -6 to 6
- inputs: bfloat16 [4096, 16384], P('col', 'row'), may hold values from -6 to 6
- gate_pre: bfloat16 [4096, 4096], P('row', 'col'), may hold values from -8 to 8
- up_pre: bfloat16 [4096, 4096], P('row', 'col'), may hold values from -6 to 6
- w_gate: bfloat16 [16384, 4096], P('row', 'col'), may hold values from -0.046875 to 0.046875
- w_up: bfloat16 [16384, 4096], P('row', 'col'), may hold values from -0.046875 to 0.046875
- w_down: bfloat16 [4096, 16384], P('col', 'row'), may hold values from -0.046875 to 0.046875
Outputs:
- input_grad: bfloat16 [4096, 16384], P('col', 'row')
- gate_grad: bfloat16 [16384, 4096], P('row', 'col')
- up_grad: bfloat16 [16384, 4096], P('row', 'col')
- down_grad: bfloat16 [4096, 16384], P('col', 'row')
The draws below stay inside these ranges and needn't reach their ends.
All inputs are finite; a program needn't handle non-finite values.
Results may differ from the reference program's by a relative error of at most 0.0049.
Values may be sent and summed in bfloat16 or wider, within the bound.
A program may use at most 128 MiB of HBM per device.

```python
import jax
import jax.numpy as jnp

D = 16384
FF = 4096
TOKENS = 4096


def raised(values, rng, source, target, blocks, factor):
    def block_of(axis_at):
        return (jnp.arange(values.shape[axis_at]) // (values.shape[axis_at] // blocks)).reshape((-1,) + (1,) * (values.ndim - 1 - axis_at))

    near = jax.random.permutation(rng, blocks)[block_of(target)]
    far = (block_of(target) + blocks // 2) % blocks
    return jnp.where((block_of(source) == near) | (block_of(source) == far), factor * values, values)


def block_scale(stream_key, dims, split, smallest, high):
    def one(dim, shards_of):
        heights = jax.random.uniform(jax.random.fold_in(jax.random.fold_in(stream_key, 6), dim), (shards_of,), jnp.float32, smallest / len(split), high / len(split))
        return jnp.repeat(jnp.exp(heights), dims[dim] // shards_of).reshape((-1,) + (1,) * (len(dims) - dim - 1))

    level = one(*split[0])
    for cut in split[1:]:
        level = level * one(*cut)
    return level


def normal_values(rng, shape, scale, most, split=(), kind=jnp.bfloat16):
    loudness = block_scale(rng, shape, split, -0.22, 0.18) if split else 1.0
    drawn = jax.random.normal(rng, shape, jnp.float32) * scale * loudness
    return jnp.minimum(jnp.maximum(drawn, -most), most).astype(kind)


def noise_with(key, extent, scale, reach, shards, heavy, held_as=jnp.bfloat16):
    result = scale * jax.random.normal(key, extent, jnp.float32)
    if shards:
        result = result * block_scale(key, extent, shards, -0.22, 0.18)
    return jnp.clip(raised(result, jax.random.fold_in(key, 3), *heavy), -reach, reach).astype(held_as)


def setup_inputs(seed: int = 0) -> dict:
    key_of = jax.random.split(jax.random.key(seed), 8)
    return {
        "grad_out": noise_with(key_of[0], (TOKENS, D), 1.0, 6.0, ((0, 8), (1, 32)), (1, 0, 32, 2.75)),
        "inputs": normal_values(key_of[1], (TOKENS, D), 1.0, 6.0, ((0, 8), (1, 32))),
        "gate_pre": normal_values(key_of[2], (TOKENS, FF), 1.5, 8.0, ((0, 32), (1, 8))),
        "up_pre": normal_values(key_of[3], (TOKENS, FF), 1.0, 6.0, ((0, 32), (1, 8))),
        "w_gate": normal_values(key_of[4], (D, FF), D ** -0.5, 0.046875, ((0, 32), (1, 8))),
        "w_up": normal_values(key_of[5], (D, FF), D ** -0.5, 0.046875, ((0, 32), (1, 8))),
        "w_down": normal_values(key_of[6], (FF, D), D ** -0.5, 0.046875, ((0, 8), (1, 32))),
    }


def reference(grad_out, inputs, gate_pre, up_pre, w_gate, w_up, w_down):
    grad_hidden = jnp.dot(grad_out, w_down.T, preferred_element_type=jnp.float32)
    gate_val = gate_pre.astype(jnp.float32)
    up_val = up_pre.astype(jnp.float32)
    sig_gate = jax.nn.sigmoid(gate_val)
    act_gate = gate_val * sig_gate
    hidden = (act_gate * up_val).astype(jnp.bfloat16)
    grad_gate = (grad_hidden * up_val * sig_gate * (1.0 + gate_val * (1.0 - sig_gate))).astype(jnp.bfloat16)
    grad_up = (grad_hidden * act_gate).astype(jnp.bfloat16)
    grad_scale = TOKENS ** -0.5
    down_grad = (jnp.dot(hidden.T, grad_out, preferred_element_type=jnp.float32) * grad_scale).astype(jnp.bfloat16)
    gate_grad = (jnp.dot(inputs.T, grad_gate, preferred_element_type=jnp.float32) * grad_scale).astype(jnp.bfloat16)
    up_grad = (jnp.dot(inputs.T, grad_up, preferred_element_type=jnp.float32) * grad_scale).astype(jnp.bfloat16)
    total = jnp.dot(grad_gate, w_gate.T, preferred_element_type=jnp.float32)
    total = total + jnp.dot(grad_up, w_up.T, preferred_element_type=jnp.float32)
    return total.astype(jnp.bfloat16), gate_grad, up_grad, down_grad
```

```python
import functools

import jax
import jax.numpy as jnp
from jax import lax
from jax.experimental import pallas as pl
from jax.experimental.pallas import tpu as pltpu
from jax.sharding import PartitionSpec as P

MESH = pl.DeviceIdType.MESH
F32, BF16 = jnp.float32, jnp.bfloat16
B = 512
ROWS = 128
ORDER = ((0, 0), (1, 0), (0, 1), (0, 3), (0, 2), (1, 1), (1, 3), (1, 2))
AT = {where: place for place, where in enumerate(ORDER)}
NT = (((1,), (1,)), ((), ()))
TN = (((0,), (0,)), ((), ()))


def kernel(
    go_ref, in_ref, gate_ref, up_ref, wg_ref, wu_ref, wd_ref,
    ig_ref, gg_ref, ug_ref, dg_ref,
    go, inp, act, gh, part, own, core_in,
    y_out, y_mid, y_in, h_sum, h_in, x_out, x_in, acc,
    send_sem, recv_sem,
):
    row, col = lax.axis_index("row"), lax.axis_index("col")
    k, h, y = lax.rem(row, 2), lax.rem(row // 2, 4), row // 8
    x, z = lax.rem(col, 4), col // 4

    def up_to(v, n):
        return lax.rem(v, n)

    def row_of(y_, h_, k_):
        return (y_ * 4 + h_) * 2 + k_

    x_right, x_left, x_far = ((row, z * 4 + up_to(x + d, 4)) for d in (1, 3, 2))
    z_pair = (row, (1 - z) * 4 + x)
    y_next, y_prev, y_far = (up_to(y + d, 4) for d in (1, 3, 2))
    y_right, y_left = ((row_of(v, h, k), col) for v in (y_next, y_prev))
    h_next, h_prev, h_far = (up_to(h + d, 4) for d in (1, 3, 2))
    h_right, h_left, h_over = ((row_of(y, v, k), col) for v in (h_next, h_prev, h_far))
    twin = (row_of(y, h, 1 - k), col)
    friends = (x_right, x_left, x_far, z_pair, y_right, y_left, h_right, h_left, h_over, twin)

    barrier = pltpu.get_barrier_semaphore()
    for friend in friends:
        pl.semaphore_signal(barrier, inc=1, device_id=friend, device_id_type=MESH)
    pl.semaphore_wait(barrier, len(friends))

    copies = []

    def send(src, dst, to):
        n = len(copies)
        copy = pltpu.make_async_remote_copy(
            src_ref=src, dst_ref=dst, send_sem=send_sem.at[n], recv_sem=recv_sem.at[n],
            device_id=to, device_id_type=MESH,
        )
        copy.start()
        copies.append([copy, False])
        return n

    def arrived(*ns):
        for n in ns:
            copies[n][0].wait_recv()

    def gone(*ns):
        for n in ns:
            if not copies[n][1]:
                copies[n][0].wait_send()
                copies[n][1] = True

    first, second = pl.ds(0, B // 2), pl.ds(B // 2, B // 2)

    def gather_own(src, buf):
        return (
            send(src, buf.at[AT[0, 3]], x_right),
            send(src, buf.at[AT[0, 1]], x_left),
            send(src, buf.at[AT[1, 0]], z_pair),
        )

    def gather_pair(buf):
        return (
            send(buf.at[AT[1, 0]], buf.at[AT[1, 3]], x_right),
            send(buf.at[AT[1, 0]], buf.at[AT[1, 1]], x_left),
        )

    def gather_far(buf, plane):
        return (
            send(buf.at[AT[plane, 3], first], buf.at[AT[plane, 2], first], x_right),
            send(buf.at[AT[plane, 1], second], buf.at[AT[plane, 2], second], x_left),
        )

    def product(g, half, to):
        @pl.loop(0, 4)
        def _(i):
            place = g * 4 + half * 2 + i // 2
            tile = go[place, pl.ds(pl.multiple_of(lax.rem(i, 2) * 256, 256), 256)]
            to[g, pl.ds(pl.multiple_of(i * 256, 256), 256)] = lax.dot_general(
                tile, wd_ref[...], NT, preferred_element_type=F32
            )

    def products(g):
        product(g, 1 - k, part)
        n = send(part.at[g], core_in.at[g], twin)
        product(g, k, own)
        return n

    def pair_sum(g, v, lo, n):
        rows = pl.ds(pl.multiple_of(v * 256 + lo, 128), n)
        return own[g, rows] + core_in[g, rows]

    lo, hi = pl.ds(0, 128), pl.ds(128, 128)

    def y_first(g):
        y_out[g, 0] = pair_sum(g, y_far, 0, 256).astype(BF16)
        a = send(y_out.at[g, 0, lo], y_mid.at[g, 0], y_right)
        b = send(y_out.at[g, 0, hi], y_mid.at[g, 1], y_left)
        y_out[g, 1, hi] = pair_sum(g, y_next, 128, 128).astype(BF16)
        c = send(y_out.at[g, 1, hi], y_in.at[g, 0, hi], y_right)
        y_out[g, 2, lo] = pair_sum(g, y_prev, 0, 128).astype(BF16)
        d = send(y_out.at[g, 2, lo], y_in.at[g, 1, lo], y_left)
        return a, b, c, d

    def y_second(g, ns):
        arrived(ns[0])
        y_out[g, 1, lo] = (pair_sum(g, y_next, 0, 128) + y_mid[g, 0].astype(F32)).astype(BF16)
        a = send(y_out.at[g, 1, lo], y_in.at[g, 0, lo], y_right)
        arrived(ns[1])
        y_out[g, 2, hi] = (pair_sum(g, y_prev, 128, 128) + y_mid[g, 1].astype(F32)).astype(BF16)
        b = send(y_out.at[g, 2, hi], y_in.at[g, 1, hi], y_left)
        return a, b

    def h_first(g, ns):
        arrived(*ns)
        h_sum[g] = pair_sum(g, y, 0, 256) + y_in[g, 0].astype(F32) + y_in[g, 1].astype(F32)

        def at(v):
            return h_sum.at[g, pl.ds(pl.multiple_of(v * 64, 64), 64)]

        return (
            send(at(h_far), h_in.at[g, 2], h_over),
            send(at(h_next), h_in.at[g, 0], h_right),
            send(at(h_prev), h_in.at[g, 1], h_left),
        )

    def gh_rows(g, y_, at_, n):
        return gh.at[pl.ds(pl.multiple_of(g * 2048 + k * 1024 + y_ * 256 + at_, 64), n)]

    def h_last(g, ns):
        arrived(*ns)
        mine = pl.ds(pl.multiple_of(h * 64, 64), 64)
        total = h_sum[g, mine] + h_in[g, 0] + h_in[g, 1] + h_in[g, 2]
        ref = gh_rows(g, y, h * 64, 64)
        ref[...] = total.astype(BF16)
        return tuple(send(ref, ref, to) for to in (h_over, h_right, h_left))

    def y_gather(g, ns):
        arrived(*ns)
        ref = gh_rows(g, y, 0, 256)
        return tuple(send(ref, ref, to) for to in (y_right, y_left, twin))

    def y_forward(g, ns):
        arrived(ns[0])
        ref = gh_rows(g, y_prev, 0, 128)
        a = send(ref, ref, y_right)
        ref = gh_rows(g, y_prev, 0, 256)
        b = send(ref, ref, twin)
        arrived(ns[1])
        ref = gh_rows(g, y_next, 128, 128)
        c = send(ref, ref, y_left)
        ref = gh_rows(g, y_next, 0, 256)
        d = send(ref, ref, twin)
        return a, b, c, d

    def y_last(g, ns):
        arrived(ns[0], ns[2])
        ref = gh_rows(g, y_far, 0, 256)
        return send(ref, ref, twin)

    def act_rows(v):
        return pl.ds(pl.multiple_of(v * 4, 4), 4)

    def block_of(place):
        other, steps = ORDER[place]
        return lax.rem(z + other, 2) * 4 + up_to(x + steps, 4)

    def gradients(place):
        block = block_of(place)

        @pl.loop(0, 32)
        def _(i):
            pair = block * 2 + i // 16
            core = lax.rem(i // 8, 2)
            rows = pl.ds(pl.multiple_of(lax.rem(i, 8) * 16, 16), 16)
            flat = pl.ds(pl.multiple_of(place * B + i * 16, 16), 16)
            gate = act[0, pair, core, rows].astype(F32)
            up = act[1, pair, core, rows].astype(F32)
            grad = gh[flat].astype(F32)
            sig = jax.nn.sigmoid(gate)
            value = gate * sig
            act[0, pair, core, rows] = (value * up).astype(BF16)
            act[1, pair, core, rows] = (grad * up * sig * (1.0 + gate * (1.0 - sig))).astype(BF16)
            gh[flat] = (grad * value).astype(BF16)

    def input_terms(place, store):
        block = block_of(place)

        @pl.loop(0, 2)
        def _(i):
            grad_gate = act[1, block * 2 + i].reshape(256, B)
            grad_up = gh[pl.ds(pl.multiple_of(place * B + i * 256, 256), 256)]
            store(
                pl.ds(pl.multiple_of(i * 256, 256), 256),
                lax.dot_general(grad_gate, wg_ref[...], NT, preferred_element_type=F32)
                + lax.dot_general(grad_up, wu_ref[...], NT, preferred_element_type=F32),
            )

    def kept(n):
        def store(rows, value):
            acc[n, rows] = value
        return store

    def sent(n):
        def store(rows, value):
            x_out[n, rows] = value.astype(BF16)
        return store

    def sent_with(n, m):
        def store(rows, value):
            x_out[n, rows] = (value + x_in[m, rows].astype(F32)).astype(BF16)
        return store

    def weight_grads(places, which, out_ref, last):
        scale = (8 * B) ** -0.5

        @pl.loop(0, 2)
        def _(i):
            rows = pl.ds(pl.multiple_of(i * 256, 256), 256)
            total = None
            for place in places:
                block = block_of(place)
                if which == 0:
                    left = act[0, pl.ds(block * 2, 2), :, :, rows].reshape(B, 256)
                    right = go[place]
                else:
                    left = inp[place, :, rows]
                    if which == 1:
                        right = act[1, pl.ds(block * 2, 2)].reshape(B, B)
                    else:
                        right = gh[pl.ds(place * B, B)]
                term = lax.dot_general(left, right, TN, preferred_element_type=F32)
                total = term if total is None else total + term
            if last:
                if len(places) < 8:
                    total = total + acc[2, rows]
                out_ref[rows] = (total * scale).astype(BF16)
            else:
                acc[2, rows] = total

    go_own = gather_own(go_ref, go)
    go[AT[0, 0]] = go_ref[...]
    inp[AT[0, 0]] = in_ref[...]
    mine = y * 4 + h
    act[0, mine, k] = gate_ref[...]
    act[1, mine, k] = up_ref[...]
    arrived(go_own[0], go_own[1])
    go_far = gather_far(go, 0)
    arrived(go_own[2])
    go_pair = gather_pair(go)
    ref = act.at[:, mine, k]
    act_h = send(ref, ref, h_right), send(ref, ref, h_left)

    core0 = products(0)
    arrived(*act_h)
    ref = act.at[0, y * 4 + h_prev, k]
    act_h2 = send(ref, ref, h_right)
    ref = act.at[1, y * 4 + h_next, k]
    act_h3 = send(ref, ref, h_left)
    arrived(core0)
    ya0 = y_first(0)
    yb0 = y_second(0, ya0)
    arrived(*go_far)
    go_last = send(go.at[AT[0, 2]], go.at[AT[1, 2]], z_pair)
    arrived(act_h2, act_h3)
    ref = act.at[:, act_rows(y), k]
    act_y = send(ref, ref, y_right), send(ref, ref, y_left)
    ha0 = h_first(0, (ya0[2], ya0[3]) + yb0)
    arrived(*go_pair)
    in_own = gather_own(in_ref, inp)
    arrived(go_last)
    core1 = products(1)
    hb0 = h_last(0, ha0)
    arrived(*act_y)
    ref = act.at[0, act_rows(y_prev), k]
    act_y2 = send(ref, ref, y_right)
    ref = act.at[1, act_rows(y_next), k]
    act_y3 = send(ref, ref, y_left)
    arrived(core1)
    ya1 = y_first(1)
    yc0 = y_gather(0, hb0)
    arrived(in_own[0], in_own[1])
    in_far = gather_far(inp, 0)
    arrived(in_own[2])
    in_pair = gather_pair(inp)
    yb1 = y_second(1, ya1)
    yd0 = y_forward(0, yc0)
    twins = []
    for v in (y, y_prev, y_next):
        ref = act.at[:, act_rows(v), k]
        twins.append(send(ref, ref, twin))
    ha1 = h_first(1, (ya1[2], ya1[3]) + yb1)
    ye0 = y_last(0, yd0)
    arrived(act_y2, act_y3)
    ref = act.at[:, act_rows(y_far), k]
    twins.append(send(ref, ref, twin))
    hb1 = h_last(1, ha1)
    arrived(yc0[2], yd0[1], yd0[3], ye0)
    arrived(*twins)
    yc1 = y_gather(1, hb1)
    arrived(*in_pair)
    in_far1 = gather_far(inp, 1)
    gone(*act_h, act_h2, act_h3, *act_y, act_y2, act_y3, *twins)
    gone(*hb0, *yc0, *yd0, ye0)
    for place in (2, 3):
        gradients(place)
        input_terms(place, sent(place - 2))
        if place == 2:
            x0 = send(x_out.at[0], x_in.at[0], x_right)
        else:
            x1 = send(x_out.at[1], x_in.at[1], x_left)
    yd1 = y_forward(1, yc1)
    for place in (0, 1):
        gradients(place)
        input_terms(place, kept(place))
    ye1 = y_last(1, yd1)
    weight_grads((0, 1, 2, 3), 0, dg_ref, False)
    arrived(yc1[2], yd1[1], yd1[3], ye1)
    gone(*hb1, *yc1, *yd1, ye1)
    gradients(7)
    input_terms(7, sent(2))
    x2 = send(x_out.at[2], x_in.at[2], z_pair)
    gradients(5)
    input_terms(5, sent(3))
    x3 = send(x_out.at[3], x_in.at[3], x_right)
    gradients(6)
    input_terms(6, sent(4))
    x4 = send(x_out.at[4], x_in.at[4], x_left)
    gradients(4)
    arrived(x2)
    input_terms(4, sent_with(5, 2))
    x5 = send(x_out.at[5], x_in.at[5], x_far)
    weight_grads((4, 5, 6, 7), 0, dg_ref, True)
    arrived(x3, x4)
    for i in range(2):
        rows = pl.ds(i * 256, 256)
        x_out[6, rows] = (acc[1, rows] + x_in[3, rows].astype(F32) + x_in[4, rows].astype(F32)).astype(BF16)
    x6 = send(x_out.at[6], x_in.at[6], z_pair)
    arrived(*in_far, *in_far1)
    weight_grads(tuple(range(8)), 1, gg_ref, True)
    weight_grads(tuple(range(8)), 2, ug_ref, True)
    arrived(x0, x1, x5, x6)
    for i in range(2):
        rows = pl.ds(i * 256, 256)
        total = acc[0, rows]
        for n in (0, 1, 5, 6):
            total = total + x_in[n, rows].astype(F32)
        ig_ref[rows] = total.astype(BF16)
    gone(*range(len(copies)))


def per_device(*args):
    vmem = pl.BlockSpec(memory_space=pltpu.VMEM)
    block = jax.ShapeDtypeStruct((B, B), BF16)
    return tuple(pl.pallas_call(
        kernel,
        name="slab_backward",
        out_shape=(block,) * 4,
        in_specs=[vmem] * 7,
        out_specs=(vmem,) * 4,
        scratch_shapes=[
            pltpu.VMEM((8, B, B), BF16),
            pltpu.VMEM((8, B, B), BF16),
            pltpu.VMEM((2, 16, 2, ROWS, B), BF16),
            pltpu.VMEM((8 * B, B), BF16),
            pltpu.VMEM((2, 2 * B, B), F32),
            pltpu.VMEM((2, 2 * B, B), F32),
            pltpu.VMEM((2, 2 * B, B), F32),
            pltpu.VMEM((2, 3, 256, B), BF16),
            pltpu.VMEM((2, 2, 128, B), BF16),
            pltpu.VMEM((2, 2, 256, B), BF16),
            pltpu.VMEM((2, 256, B), F32),
            pltpu.VMEM((2, 3, 64, B), F32),
            pltpu.VMEM((7, B, B), BF16),
            pltpu.VMEM((7, B, B), BF16),
            pltpu.VMEM((3, B, B), F32),
            pltpu.SemaphoreType.DMA((96,)),
            pltpu.SemaphoreType.DMA((96,)),
        ],
        compiler_params=pltpu.CompilerParams(
            collective_id=0, has_side_effects=True, vmem_limit_bytes=60 * 1024 * 1024
        ),
        cost_estimate=pl.CostEstimate(flops=12 * 4096 * B * B, bytes_accessed=12 * B * B, transcendentals=4096 * B),
    )(*args))


def solution(mesh):
    placed = (
        P("col", "row"),
        P("col", "row"),
        P("row", "col"),
        P("row", "col"),
        P("row", "col"),
        P("row", "col"),
        P("col", "row"),
    )
    return jax.shard_map(
        per_device,
        mesh=mesh,
        in_specs=placed,
        out_specs=(P("col", "row"), P("row", "col"), P("row", "col"), P("col", "row")),
        check_vma=False,
    )
```

```python
import functools

import jax
import jax.numpy as jnp
from jax import lax
from jax.experimental import pallas as pl
from jax.experimental.pallas import tpu as pltpu
from jax.sharding import PartitionSpec as P

MESH = pl.DeviceIdType.MESH
F32, BF16 = jnp.float32, jnp.bfloat16
B = 512
ROWS = 128
ORDER = ((0, 1), (0, 3), (1, 1), (1, 3), (0, 2), (1, 2), (0, 0), (1, 0))
AT = {where: place for place, where in enumerate(ORDER)}
GROUPS = 4
HALF = 8 * B // GROUPS // 2
YR = HALF // 4
HR = YR // 4
FAR = "go4"
INS = ("in0", "in3", "in1", "in2", "in4")
ACTS = ("a0", "a1", "a2", "a3", "bp", "bn", "bf", "cp", "cn", "cf", "t0", "t1", "t2")
SCHEDULE = (
    "go1", "go0", "go3", "a0", "a1", "P0", "Y0", "P3", "Y3", "a3",
    "in1", "go2", "Z0", "a2", "go4", "bp", "P1", "bn", "Y1", "t0",
    "in0", "Z1", "P2", "H0", "bf", "Y2", "H1", "in3", "Z2", "cn",
    "I1", "cp", "H2", "J1", "in4", "cf", "in2", "t1", "I0", "K1",
    "I2", "Z3", "t2", "J0", "L1", "H3", "J2", "R1", "u11a", "u13b",
    "u11b", "K0", "u13a", "K2", "I3", "L0", "L2", "R0", "u01a", "R2",
    "u12a", "u03b", "u12b", "J3", "u01b", "u03a", "w0", "K3", "d0", "v02b",
    "L3", "R3", "u10a", "s1a", "u02b", "v02a", "u10b", "s1b", "u02a", "u00b",
    "g0", "u00a", "w1", "d1", "g1", "s0b", "s0a",
)
NT = (((1,), (1,)), ((), ()))
TN = (((0,), (0,)), ((), ()))


def kernel(
    go_hbm, in_hbm, gate_hbm, up_hbm, wg_hbm, wu_hbm, wd_hbm,
    ig_hbm, gg_hbm, ug_hbm, dg_hbm,
    weights_in, results, go, inp, act, gh, part, own, core_in,
    y_out, y_mid, y_in, h_sum, h_in, x_out, x_in, acc, held,
    send_sem, recv_sem, local_sem,
):
    row, col = lax.axis_index("row"), lax.axis_index("col")
    k, h, y = lax.rem(row, 2), lax.rem(row // 2, 4), row // 8
    x, z = lax.rem(col, 4), col // 4

    def row_of(y_, h_, k_):
        return (y_ * 4 + h_) * 2 + k_

    x_right, x_left, x_far = ((row, z * 4 + lax.rem(x + d, 4)) for d in (1, 3, 2))
    z_pair = (row, (1 - z) * 4 + x)
    y_next, y_prev, y_far = (lax.rem(y + d, 4) for d in (1, 3, 2))
    y_right, y_left = ((row_of(v, h, k), col) for v in (y_next, y_prev))
    h_next, h_prev, h_far = (lax.rem(h + d, 4) for d in (1, 3, 2))
    h_right, h_left, h_over = ((row_of(y, v, k), col) for v in (h_next, h_prev, h_far))
    twin = (row_of(y, h, 1 - k), col)
    friends = (x_right, x_left, x_far, z_pair, y_right, y_left, h_right, h_left, h_over, twin)

    mine = y * 4 + h
    loads = [
        pltpu.make_async_copy(src, dst, local_sem.at[n])
        for n, (src, dst) in enumerate((
            (go_hbm, go.at[AT[0, 0]]),
            (gate_hbm, act.at[0, mine, k]),
            (up_hbm, act.at[1, mine, k]),
            (wd_hbm, weights_in.at[2]),
            (in_hbm, inp.at[AT[0, 0]]),
            (wg_hbm, weights_in.at[0]),
            (wu_hbm, weights_in.at[1]),
        ))
    ]
    for load in loads:
        load.start()
    wg_ref, wu_ref, wd_ref = (weights_in.at[n] for n in range(3))
    ig_ref, gg_ref, ug_ref, dg_ref = (results.at[n] for n in range(4))

    barrier = pltpu.get_barrier_semaphore()
    for friend in friends:
        pl.semaphore_signal(barrier, inc=1, device_id=friend, device_id_type=MESH)
    pl.semaphore_wait(barrier, len(friends))

    for load in loads[:3]:
        load.wait()
    copies = []
    made = {}
    tasks = {}

    def send(src, dst, to):
        n = len(copies)
        copy = pltpu.make_async_remote_copy(
            src_ref=src, dst_ref=dst, send_sem=send_sem.at[n], recv_sem=recv_sem.at[n],
            device_id=to, device_id_type=MESH,
        )
        copy.start()
        copies.append([copy, False, False])
        return n

    waited = [True] * 3 + [False] * 4

    def loaded(n):
        if not waited[n]:
            loads[n].wait()
            waited[n] = True

    def arrived(*ns):
        for n in ns:
            if not copies[n][2]:
                copies[n][0].wait_recv()
                copies[n][2] = True

    def gone(*ns):
        for n in ns:
            if not copies[n][1]:
                copies[n][0].wait_send()
                copies[n][1] = True

    def task(name):
        def add(run):
            def step():
                made[name] = run()
            tasks[name] = step
            return run
        return add

    def at(start, n, step):
        return pl.ds(pl.multiple_of(start, step), n)

    first, second = pl.ds(0, B // 2), pl.ds(B // 2, B // 2)

    saves = []

    def save(n, rows=slice(None)):
        copy = pltpu.make_async_copy(
            results.at[n, rows], (ig_hbm, gg_hbm, ug_hbm, dg_hbm)[n].at[rows], local_sem.at[len(loads) + len(saves)]
        )
        copy.start()
        saves.append(copy)

    def gather(name, load, buf):
        src = buf.at[AT[0, 0]]

        @task(name + "0")
        def _():
            loaded(load)
            return (
                send(src, buf.at[AT[0, 3]], x_right),
                send(src, buf.at[AT[0, 1]], x_left),
            )

        @task(name + "1")
        def _():
            loaded(load)
            return (send(src, buf.at[AT[1, 0]], z_pair),)

        def far(plane):
            return (
                send(buf.at[AT[plane, 3], first], buf.at[AT[plane, 2], first], x_right),
                send(buf.at[AT[plane, 1], second], buf.at[AT[plane, 2], second], x_left),
            )

        @task(name + "2")
        def _():
            arrived(*made[name + "0"])
            return far(0)

        @task(name + "3")
        def _():
            arrived(*made[name + "1"])
            return (
                send(buf.at[AT[1, 0]], buf.at[AT[1, 3]], x_right),
                send(buf.at[AT[1, 0]], buf.at[AT[1, 1]], x_left),
            )

        @task(name + "4")
        def _():
            arrived(*made[name + "3"])
            return far(1)

        @task(name + "z")
        def _():
            arrived(*made[name + "2"])
            return (send(buf.at[AT[0, 2]], buf.at[AT[1, 2]], z_pair),)

    gather("go", 0, go)
    gather("in", 4, inp)

    @task("a0")
    def _():
        ref = act.at[:, mine, k]
        return send(ref, ref, h_right), send(ref, ref, h_left)

    def act_to_y(h_):
        ref = act.at[:, y * 4 + h_, k]
        return send(ref, ref, y_right), send(ref, ref, y_left)

    def act_on_y(h_):
        ref = act.at[0, y_prev * 4 + h_, k]
        n = send(ref, ref, y_right)
        ref = act.at[1, y_next * 4 + h_, k]
        return n, send(ref, ref, y_left)

    @task("a1")
    def _():
        return act_to_y(h)

    @task("a2")
    def _():
        arrived(*made["a0"])
        ref = act.at[0, y * 4 + h_prev, k]
        n = send(ref, ref, h_right)
        ref = act.at[1, y * 4 + h_next, k]
        return n, send(ref, ref, h_left)

    @task("a3")
    def _():
        arrived(*made["a1"])
        return act_on_y(h)

    for name, h_, source in (("p", h_prev, "a0"), ("n", h_next, "a0"), ("f", h_far, "a2")):
        def pair(name=name, h_=h_, source=source):
            @task("b" + name)
            def _():
                arrived(*made[source])
                return act_to_y(h_)

            @task("c" + name)
            def _():
                arrived(*made["b" + name])
                return act_on_y(h_)
        pair()

    def act_twin(y_):
        ref = act.at[:, at(y_ * 4, 4, 4), k]
        return send(ref, ref, twin)

    @task("t0")
    def _():
        arrived(*made["a0"], *made["a2"])
        return (act_twin(y),)

    @task("t1")
    def _():
        arrived(*made["a1"], *made["bp"], *made["bn"], *made["bf"])
        return act_twin(y_prev), act_twin(y_next)

    @task("t2")
    def _():
        arrived(*made["a3"], *made["cp"], *made["cn"], *made["cf"])
        return (act_twin(y_far),)

    needs = (("go0",), ("go3",), ("go2", FAR), ("go1",))

    def product(g, half, to):
        step = min(256, HALF)

        @pl.loop(0, HALF // step)
        def _(i):
            place = g * 2 + half
            tile = go[place, at(i * step, step, step)]
            to[g, at(i * step, step, step)] = lax.dot_general(
                tile, wd_ref[...], NT, preferred_element_type=F32
            )

    def pair_sum(g, v, lo, n):
        rows = at(v * YR + lo, n, 64)
        return own[g, rows] + core_in[g, rows]

    lo, hi = pl.ds(0, YR // 2), pl.ds(YR // 2, YR // 2)

    def gh_rows(g, y_, start, n):
        return gh.at[at(g * 2 * HALF + k * HALF + y_ * YR + start, n, HR)]

    def summed(g):
        t = str(g)

        @task("P" + t)
        def _():
            for name in needs[g]:
                arrived(*made[name])
            loaded(3)
            product(g, 1 - k, part)
            n = send(part.at[g], core_in.at[g], twin)
            product(g, k, own)
            return (n,)

        @task("Y" + t)
        def _():
            arrived(*made["P" + t])
            y_out[g, 0] = pair_sum(g, y_far, 0, YR).astype(BF16)
            a = send(y_out.at[g, 0, lo], y_mid.at[g, 0], y_right)
            b = send(y_out.at[g, 0, hi], y_mid.at[g, 1], y_left)
            y_out[g, 1, hi] = pair_sum(g, y_next, YR // 2, YR // 2).astype(BF16)
            c = send(y_out.at[g, 1, hi], y_in.at[g, 0, hi], y_right)
            y_out[g, 2, lo] = pair_sum(g, y_prev, 0, YR // 2).astype(BF16)
            d = send(y_out.at[g, 2, lo], y_in.at[g, 1, lo], y_left)
            return a, b, c, d

        @task("Z" + t)
        def _():
            a, b, c, d = made["Y" + t]
            arrived(a)
            y_out[g, 1, lo] = (pair_sum(g, y_next, 0, YR // 2) + y_mid[g, 0].astype(F32)).astype(BF16)
            e = send(y_out.at[g, 1, lo], y_in.at[g, 0, lo], y_right)
            arrived(b)
            y_out[g, 2, hi] = (pair_sum(g, y_prev, YR // 2, YR // 2) + y_mid[g, 1].astype(F32)).astype(BF16)
            f = send(y_out.at[g, 2, hi], y_in.at[g, 1, hi], y_left)
            h_sum[g] = pair_sum(g, y, 0, YR)
            return c, d, e, f

        @task("H" + t)
        def _():
            arrived(*made["Z" + t])
            h_sum[g] = h_sum[g] + y_in[g, 0].astype(F32) + y_in[g, 1].astype(F32)

            def piece(v):
                return h_sum.at[g, at(v * HR, HR, HR)]

            return (
                send(piece(h_far), h_in.at[g, 2], h_over),
                send(piece(h_next), h_in.at[g, 0], h_right),
                send(piece(h_prev), h_in.at[g, 1], h_left),
            )

        @task("I" + t)
        def _():
            arrived(*made["H" + t])
            total = h_sum[g, at(h * HR, HR, HR)] + h_in[g, 0] + h_in[g, 1] + h_in[g, 2]
            ref = gh_rows(g, y, h * HR, HR)
            ref[...] = total.astype(BF16)
            return tuple(send(ref, ref, to) for to in (h_over, h_right, h_left))

        @task("J" + t)
        def _():
            arrived(*made["I" + t])
            ref = gh_rows(g, y, 0, YR)
            return tuple(send(ref, ref, to) for to in (y_right, y_left, twin))

        @task("K" + t)
        def _():
            a, b, c = made["J" + t]
            arrived(a)
            ref = gh_rows(g, y_prev, 0, YR // 2)
            d = send(ref, ref, y_right)
            ref = gh_rows(g, y_prev, 0, YR)
            e = send(ref, ref, twin)
            arrived(b)
            ref = gh_rows(g, y_next, YR // 2, YR // 2)
            f = send(ref, ref, y_left)
            ref = gh_rows(g, y_next, 0, YR)
            i = send(ref, ref, twin)
            return d, f, c, e, i

        @task("L" + t)
        def _():
            d, f, c, e, i = made["K" + t]
            arrived(d, f)
            ref = gh_rows(g, y_far, 0, YR)
            return c, e, i, send(ref, ref, twin)

        @task("R" + t)
        def _():
            arrived(*made["L" + t])
            for name in ("I", "J", "K", "L"):
                gone(*made[name + t])
            for name in ACTS:
                arrived(*made[name])
                gone(*made[name])

    for g in range(GROUPS):
        summed(g)

    def block_of(place):
        other, steps = ORDER[place]
        return lax.rem(z + other, 2) * 4 + lax.rem(x + steps, 4)

    def gradients(place, half):
        block = block_of(place)

        @pl.loop(half * 16, half * 16 + 16, unroll=2)
        def _(i):
            pair = block * 2 + i // 16
            core = lax.rem(i // 8, 2)
            rows = at(lax.rem(i, 8) * 16, 16, 16)
            flat = at(place * B + i * 16, 16, 16)
            gate = act[0, pair, core, rows].astype(F32)
            up = act[1, pair, core, rows].astype(F32)
            grad = gh[flat].astype(F32)
            sig = 0.5 * jnp.tanh(0.5 * gate) + 0.5
            value = gate * sig
            act[0, pair, core, rows] = (value * up).astype(BF16)
            act[1, pair, core, rows] = (grad * up * sig * (1.0 + gate * (1.0 - sig))).astype(BF16)
            gh[flat] = (grad * value).astype(BF16)

    def input_terms(place, half):
        loaded(5)
        loaded(6)
        grad_gate = act[1, block_of(place) * 2 + half].reshape(256, B)
        grad_up = gh[pl.ds(place * B + half * 256, 256)]
        gate_term = lax.dot_general(grad_gate, wg_ref[...], NT, preferred_element_type=F32)
        return gate_term + lax.dot_general(grad_up, wu_ref[...], NT, preferred_element_type=F32)

    halves = ((0, "a", first), (1, "b", second))

    def out(name, n, where, to):
        for half, t, rows in halves:
            def one(half=half, t=t, rows=rows):
                @task("u" + name + t)
                def _():
                    gradients(AT[where], half)
                    x_out[n, rows] = input_terms(AT[where], half).astype(BF16)
                    return (send(x_out.at[n, rows], x_in.at[n, rows], to),)
            one()

    out("01", 0, (0, 1), x_right)
    out("03", 1, (0, 3), x_left)
    out("11", 3, (1, 1), x_right)
    out("13", 4, (1, 3), x_left)
    out("12", 2, (1, 2), z_pair)

    def rest(half, t, rows):
        @task("v02" + t)
        def _():
            gradients(AT[0, 2], half)

        @task("u02" + t)
        def _():
            arrived(*made["u12" + t])
            total = input_terms(AT[0, 2], half) + x_in[2, rows].astype(F32)
            x_out[5, rows] = total.astype(BF16)
            return (send(x_out.at[5, rows], x_in.at[5, rows], x_far),)

        @task("u00" + t)
        def _():
            gradients(AT[0, 0], half)
            acc[0, rows] = input_terms(AT[0, 0], half)

        @task("u10" + t)
        def _():
            gradients(AT[1, 0], half)
            acc[1, rows] = input_terms(AT[1, 0], half)

        @task("s1" + t)
        def _():
            arrived(*made["u11" + t], *made["u13" + t])
            total = acc[1, rows] + x_in[3, rows].astype(F32) + x_in[4, rows].astype(F32)
            x_out[6, rows] = total.astype(BF16)
            return (send(x_out.at[6, rows], x_in.at[6, rows], z_pair),)

        @task("s0" + t)
        def _():
            arrived(*made["u01" + t], *made["u03" + t], *made["u02" + t], *made["s1" + t])
            total = acc[0, rows]
            for n in (0, 1, 5, 6):
                total = total + x_in[n, rows].astype(F32)
            ig_ref[rows] = total.astype(BF16)
            return save(0, rows)

    for half, t, rows in halves:
        rest(half, t, rows)

    def weight_grads(places, which, out_ref, last):
        scale = (8 * B) ** -0.5

        @pl.loop(0, 2)
        def _(i):
            rows = at(i * 256, 256, 256)
            total = None
            for place in places:
                block = block_of(place)
                if which == 0:
                    left = act[0, pl.ds(block * 2, 2), :, :, rows].reshape(B, 256)
                    right = go[place]
                else:
                    left = inp[place, :, rows]
                    if which == 1:
                        right = act[1, pl.ds(block * 2, 2)].reshape(B, B)
                    else:
                        right = gh[pl.ds(place * B, B)]
                term = lax.dot_general(left, right, TN, preferred_element_type=F32)
                total = term if total is None else total + term
            if last:
                out_ref[rows] = ((total + held[which, rows]) * scale).astype(BF16)
            else:
                held[which, rows] = total

    def weights(name, which, out_ref):
        @task(name + "0")
        def _():
            if which:
                for n in INS[:2]:
                    arrived(*made[n])
            weight_grads((0, 1, 2, 3), which, out_ref, False)

        @task(name + "1")
        def _():
            if which:
                for n in INS:
                    arrived(*made[n])
            weight_grads((4, 5, 6, 7), which, out_ref, True)
            save((3, 1, 2)[which])

    weights("d", 0, dg_ref)
    weights("g", 1, gg_ref)
    weights("w", 2, ug_ref)

    for name in SCHEDULE:
        tasks[name]()
    arrived(*range(len(copies)))
    gone(*range(len(copies)))
    for copy in saves:
        copy.wait()


def handed_on(*refs):
    held, sems = refs[8:]
    ins = [pltpu.make_async_copy(refs[n], held.at[n], sems.at[n]) for n in range(4)]
    outs = [pltpu.make_async_copy(held.at[n], refs[4 + n], sems.at[4 + n]) for n in range(4)]
    for move in ins:
        move.start()
    for n in range(4):
        ins[n].wait()
        outs[n].start()
    for move in outs:
        move.wait()


def per_device(*args):
    hbm = pl.BlockSpec(memory_space=pl.ANY)
    block = jax.ShapeDtypeStruct((B, B), BF16)
    made = pl.pallas_call(
        kernel,
        name="slab_backward",
        out_shape=(block,) * 4,
        in_specs=[hbm] * 7,
        out_specs=(hbm,) * 4,
        scratch_shapes=[
            pltpu.VMEM((3, B, B), BF16),
            pltpu.VMEM((4, B, B), BF16),
            pltpu.VMEM((8, B, B), BF16),
            pltpu.VMEM((8, B, B), BF16),
            pltpu.VMEM((2, 16, 2, ROWS, B), BF16),
            pltpu.VMEM((8 * B, B), BF16),
            pltpu.VMEM((GROUPS, HALF, B), F32),
            pltpu.VMEM((GROUPS, HALF, B), F32),
            pltpu.VMEM((GROUPS, HALF, B), F32),
            pltpu.VMEM((GROUPS, 3, YR, B), BF16),
            pltpu.VMEM((GROUPS, 2, YR // 2, B), BF16),
            pltpu.VMEM((GROUPS, 2, YR, B), BF16),
            pltpu.VMEM((GROUPS, YR, B), F32),
            pltpu.VMEM((GROUPS, 3, HR, B), F32),
            pltpu.VMEM((7, B, B), BF16),
            pltpu.VMEM((7, B, B), BF16),
            pltpu.VMEM((2, B, B), F32),
            pltpu.VMEM((3, B, B), F32),
            pltpu.SemaphoreType.DMA((160,)),
            pltpu.SemaphoreType.DMA((160,)),
            pltpu.SemaphoreType.DMA((12,)),
        ],
        compiler_params=pltpu.CompilerParams(
            collective_id=0, has_side_effects=True, vmem_limit_bytes=60 * 1024 * 1024
        ),
        cost_estimate=pl.CostEstimate(flops=12 * 4096 * B * B, bytes_accessed=12 * B * B, transcendentals=4096 * B),
    )(*args)
    return tuple(pl.pallas_call(
        handed_on,
        name="hand_on",
        out_shape=(block,) * 4,
        in_specs=[hbm] * 4,
        out_specs=(hbm,) * 4,
        scratch_shapes=[pltpu.VMEM((4, B, B), BF16), pltpu.SemaphoreType.DMA((8,))],
        compiler_params=pltpu.CompilerParams(vmem_limit_bytes=60 * 1024 * 1024),
    )(*made))


def solution(mesh):
    placed = (
        P("col", "row"),
        P("col", "row"),
        P("row", "col"),
        P("row", "col"),
        P("row", "col"),
        P("row", "col"),
        P("col", "row"),
    )
    return jax.shard_map(
        per_device,
        mesh=mesh,
        in_specs=placed,
        out_specs=(P("col", "row"), P("row", "col"), P("row", "col"), P("col", "row")),
        check_vma=False,
    )
```

```python
import functools

import jax
import jax.numpy as jnp
from jax import lax
from jax.experimental import pallas as pl
from jax.experimental.pallas import tpu as pltpu
from jax.sharding import PartitionSpec as P

MESH = pl.DeviceIdType.MESH
F32, BF16 = jnp.float32, jnp.bfloat16
B = 512
ROWS = 128
ORDER = ((0, 1), (0, 3), (1, 1), (1, 3), (0, 2), (1, 2), (0, 0), (1, 0))
AT = {where: place for place, where in enumerate(ORDER)}
GROUPS = 4
HALF = 8 * B // GROUPS // 2
YR = HALF // 4
HR = YR // 4
X_RING, FAR_BY_X = False, False
Y_DIRECT = False
Y_TYPE, H_TYPE = BF16, BF16
RING_IN, RING_OUT = False, False
INS = ("in0a", "in0b", "in3a", "in3b", "in1a", "in1b", "in2a", "in2b", "in4a", "in4b")
ACTS = ("a0", "a1", "a2", "a3", "bp", "bn", "bf", "cp", "cn", "cf", "t0", "t1", "t2")
SCHEDULE = (
    "go1b", "a1", "go0a", "go0b", "go1a", "a3", "go3b", "a0", "P3", "go3a",
    "P0", "Y3", "Y0", "Z3", "in1b", "in1a", "go4b", "go2a", "Z0", "P1",
    "go2b", "bp", "a2", "go4a", "Y1", "Z1", "in0b", "bn", "in0a", "P2",
    "H1", "cp", "in3a", "Y2", "I1", "bf", "Z2", "H0", "in3b", "in2a",
    "H3", "F1", "t0", "cn", "H2", "J1", "in4a", "in2b", "I0", "cf",
    "t1", "I2", "F0", "K1", "J0", "F2", "t2", "I3", "L1", "in4b",
    "J2", "R1", "u13", "K0", "u11", "F3", "K2", "L0", "R0", "u01",
    "L2", "J3", "R2", "v12", "u12b", "u03", "K3", "d0", "u12a", "w0",
    "L3", "R3", "u10", "s1b", "s1a", "v02", "u02b", "u00", "g0", "u02a",
    "g1", "w1", "d1", "s0b", "s0a",
)
NT = (((1,), (1,)), ((), ()))
TN = (((0,), (0,)), ((), ()))


def kernel(
    go_hbm, in_hbm, gate_hbm, up_hbm, wg_hbm, wu_hbm, wd_hbm,
    ig_hbm, gg_hbm, ug_hbm, dg_hbm,
    weights_in, results, go, inp, act, gh, part, own, core_in,
    y_out, y_in, h_sum, h_out, h_in, x_out, x_in, acc, held,
    send_sem, recv_sem, local_sem,
):
    row, col = lax.axis_index("row"), lax.axis_index("col")
    k, h, y = lax.rem(row, 2), lax.rem(row // 2, 4), row // 8
    x, z = lax.rem(col, 4), col // 4

    def row_of(y_, h_, k_):
        return (y_ * 4 + h_) * 2 + k_

    x_right, x_left, x_far = ((row, z * 4 + lax.rem(x + d, 4)) for d in (1, 3, 2))
    z_pair = (row, (1 - z) * 4 + x)
    y_next, y_prev, y_far = (lax.rem(y + d, 4) for d in (1, 3, 2))
    y_right, y_left, y_over = ((row_of(v, h, k), col) for v in (y_next, y_prev, y_far))
    h_next, h_prev, h_far = (lax.rem(h + d, 4) for d in (1, 3, 2))
    h_right, h_left, h_over = ((row_of(y, v, k), col) for v in (h_next, h_prev, h_far))
    twin = (row_of(y, h, 1 - k), col)
    friends = (x_right, x_left, z_pair, y_right, y_left, h_right, h_left, h_over, twin) + ((y_over,) if Y_DIRECT else ()) + (() if X_RING else (x_far,))

    mine = y * 4 + h
    loads = [
        pltpu.make_async_copy(src, dst, local_sem.at[n])
        for n, (src, dst) in enumerate((
            (go_hbm, go.at[AT[0, 0]]),
            (gate_hbm, act.at[0, mine, k]),
            (up_hbm, act.at[1, mine, k]),
            (wd_hbm, weights_in.at[2]),
            (in_hbm, inp.at[AT[0, 0]]),
            (wg_hbm, weights_in.at[0]),
            (wu_hbm, weights_in.at[1]),
        ))
    ]
    for load in loads:
        load.start()
    wg_ref, wu_ref, wd_ref = (weights_in.at[n] for n in range(3))
    ig_ref, gg_ref, ug_ref, dg_ref = (results.at[n] for n in range(4))

    barrier = pltpu.get_barrier_semaphore()
    for friend in friends:
        pl.semaphore_signal(barrier, inc=1, device_id=friend, device_id_type=MESH)
    pl.semaphore_wait(barrier, len(friends))

    for load in loads[:3]:
        load.wait()
    copies = []
    made = {}
    tasks = {}

    def send(src, dst, to):
        n = len(copies)
        copy = pltpu.make_async_remote_copy(
            src_ref=src, dst_ref=dst, send_sem=send_sem.at[n], recv_sem=recv_sem.at[n],
            device_id=to, device_id_type=MESH,
        )
        copy.start()
        copies.append([copy, False, False])
        return n

    waited = [True] * 3 + [False] * 4

    def loaded(n):
        if not waited[n]:
            loads[n].wait()
            waited[n] = True

    def arrived(*ns):
        for n in ns:
            if not copies[n][2]:
                copies[n][0].wait_recv()
                copies[n][2] = True

    def gone(*ns):
        for n in ns:
            if not copies[n][1]:
                copies[n][0].wait_send()
                copies[n][1] = True

    def task(name):
        def add(run):
            def step():
                made[name] = run()
            tasks[name] = step
            return run
        return add

    def at(start, n, step):
        return pl.ds(pl.multiple_of(start, step), n)

    first, second = pl.ds(0, B // 2), pl.ds(B // 2, B // 2)

    saves = []

    def save(n, rows=slice(None)):
        copy = pltpu.make_async_copy(
            results.at[n, rows], (ig_hbm, gg_hbm, ug_hbm, dg_hbm)[n].at[rows], local_sem.at[len(loads) + len(saves)]
        )
        copy.start()
        saves.append(copy)

    halves = ((0, "a", first), (1, "b", second))

    def gather(name, load, buf):
        mine = buf.at[AT[0, 0]]
        paired = buf.at[AT[1, 0]]

        def one(half, t, rows):
            def both_ways(src, plane):
                return (
                    send(src, buf.at[AT[plane, 3], rows], x_right),
                    send(src, buf.at[AT[plane, 1], rows], x_left),
                )

            def far(plane):
                if half == 0:
                    return (send(buf.at[AT[plane, 3], rows], buf.at[AT[plane, 2], rows], x_right),)
                return (send(buf.at[AT[plane, 1], rows], buf.at[AT[plane, 2], rows], x_left),)

            @task(name + "0" + t)
            def _():
                loaded(load)
                return both_ways(mine.at[rows], 0)

            @task(name + "1" + t)
            def _():
                loaded(load)
                return (send(mine.at[rows], buf.at[AT[1, 0], rows], z_pair),)

            @task(name + "2" + t)
            def _():
                arrived(made[name + "0" + t][half])
                return far(0)

            @task(name + "3" + t)
            def _():
                arrived(*made[name + "1" + t])
                return both_ways(paired.at[rows], 1)

            @task(name + "4" + t)
            def _():
                arrived(made[name + "3" + t][half])
                return far(1)

        for half, t, rows in halves:
            one(half, t, rows)

    gather("go", 0, go)
    gather("in", 4, inp)

    @task("a0")
    def _():
        ref = act.at[:, mine, k]
        return send(ref, ref, h_right), send(ref, ref, h_left)

    def act_to_y(h_):
        ref = act.at[:, y * 4 + h_, k]
        return send(ref, ref, y_right), send(ref, ref, y_left)

    def act_on_y(h_):
        ref = act.at[0, y_prev * 4 + h_, k]
        n = send(ref, ref, y_right)
        ref = act.at[1, y_next * 4 + h_, k]
        return n, send(ref, ref, y_left)

    @task("a1")
    def _():
        return act_to_y(h)

    @task("a2")
    def _():
        arrived(*made["a0"])
        ref = act.at[0, y * 4 + h_prev, k]
        n = send(ref, ref, h_right)
        ref = act.at[1, y * 4 + h_next, k]
        return n, send(ref, ref, h_left)

    @task("a3")
    def _():
        arrived(*made["a1"])
        return act_on_y(h)

    for name, h_, source in (("p", h_prev, "a0"), ("n", h_next, "a0"), ("f", h_far, "a2")):
        def pair(name=name, h_=h_, source=source):
            @task("b" + name)
            def _():
                arrived(*made[source])
                return act_to_y(h_)

            @task("c" + name)
            def _():
                arrived(*made["b" + name])
                return act_on_y(h_)
        pair()

    def act_twin(y_):
        ref = act.at[:, at(y_ * 4, 4, 4), k]
        return send(ref, ref, twin)

    @task("t0")
    def _():
        arrived(*made["a0"], *made["a2"])
        return (act_twin(y),)

    @task("t1")
    def _():
        arrived(*made["a1"], *made["bp"], *made["bn"], *made["bf"])
        return act_twin(y_prev), act_twin(y_next)

    @task("t2")
    def _():
        arrived(*made["a3"], *made["cp"], *made["cn"], *made["cf"])
        return (act_twin(y_far),)

    needs = (("go0a", "go0b"), ("go3a", "go3b"), ("go2a", "go2b", "go4a", "go4b"), ("go1a", "go1b"))

    def product(g, half, to):
        to[g] = lax.dot_general(go[g * 2 + half], wd_ref[...], NT, preferred_element_type=F32)

    def pair_sum(g, v, lo, n):
        rows = at(v * YR + lo, n, 64)
        return own[g, rows] + core_in[g, rows]

    lo, hi = pl.ds(0, YR // 2), pl.ds(YR // 2, YR // 2)

    def gh_rows(g, y_, start, n):
        return gh.at[at(g * 2 * HALF + k * HALF + y_ * YR + start, n, 16)]

    def summed(g):
        t = str(g)

        @task("P" + t)
        def _():
            for name in needs[g]:
                arrived(*made[name])
            loaded(3)
            product(g, 1 - k, part)
            n = send(part.at[g], core_in.at[g], twin)
            product(g, k, own)
            return (n,)

        @task("Y" + t)
        def _():
            arrived(*made["P" + t])
            y_out[g, 0] = pair_sum(g, y_far, 0, YR).astype(Y_TYPE)
            if Y_DIRECT:
                a = send(y_out.at[g, 0], y_in.at[g, 2], y_over)
                y_out[g, 1] = pair_sum(g, y_next, 0, YR).astype(Y_TYPE)
                b = send(y_out.at[g, 1], y_in.at[g, 0], y_right)
                y_out[g, 2] = pair_sum(g, y_prev, 0, YR).astype(Y_TYPE)
                return a, b, send(y_out.at[g, 2], y_in.at[g, 1], y_left)
            a = send(y_out.at[g, 0, lo], y_in.at[g, 2, lo], y_right)
            b = send(y_out.at[g, 0, hi], y_in.at[g, 2, hi], y_left)
            y_out[g, 1, hi] = pair_sum(g, y_next, YR // 2, YR // 2).astype(Y_TYPE)
            c = send(y_out.at[g, 1, hi], y_in.at[g, 0, hi], y_right)
            y_out[g, 2, lo] = pair_sum(g, y_prev, 0, YR // 2).astype(Y_TYPE)
            d = send(y_out.at[g, 2, lo], y_in.at[g, 1, lo], y_left)
            return a, b, c, d

        @task("Z" + t)
        def _():
            h_sum[g] = pair_sum(g, y, 0, YR)
            if Y_DIRECT:
                return made["Y" + t]
            a, b, c, d = made["Y" + t]
            arrived(a)
            y_out[g, 1, lo] = (pair_sum(g, y_next, 0, YR // 2) + y_in[g, 2, lo].astype(F32)).astype(Y_TYPE)
            e = send(y_out.at[g, 1, lo], y_in.at[g, 0, lo], y_right)
            arrived(b)
            y_out[g, 2, hi] = (pair_sum(g, y_prev, YR // 2, YR // 2) + y_in[g, 2, hi].astype(F32)).astype(Y_TYPE)
            f = send(y_out.at[g, 2, hi], y_in.at[g, 1, hi], y_left)
            return c, d, e, f

        @task("H" + t)
        def _():
            arrived(*made["Z" + t])
            total = h_sum[g] + y_in[g, 0].astype(F32) + y_in[g, 1].astype(F32)
            h_sum[g] = total + y_in[g, 2].astype(F32) if Y_DIRECT else total

            def piece(n, v):
                h_out[g, n] = h_sum[g, at(v * HR, HR, HR)].astype(H_TYPE)
                return h_out.at[g, n]

            return (
                send(piece(0, h_far), h_in.at[g, 2], h_over),
                send(piece(1, h_next), h_in.at[g, 0], h_right),
                send(piece(2, h_prev), h_in.at[g, 1], h_left),
            )

        @task("I" + t)
        def _():
            arrived(*made["H" + t])
            total = h_sum[g, at(h * HR, HR, HR)]
            for n in range(3):
                total = total + h_in[g, n].astype(F32)
            ref = gh_rows(g, y, h * HR, HR)
            ref[...] = total.astype(BF16)
            tos = (h_right, h_left) if RING_OUT else (h_over, h_right, h_left)
            return tuple(send(ref, ref, to) for to in tos)

        @task("F" + t)
        def _():
            if not RING_OUT:
                return made["I" + t]
            a, b = made["I" + t]
            arrived(a)
            ref = gh_rows(g, y, h_prev * HR, HR // 2)
            c = send(ref, ref, h_right)
            arrived(b)
            ref = gh_rows(g, y, h_next * HR + HR // 2, HR // 2)
            return a, b, c, send(ref, ref, h_left)

        @task("J" + t)
        def _():
            arrived(*made["F" + t])
            ref = gh_rows(g, y, 0, YR)
            return tuple(send(ref, ref, to) for to in (y_right, y_left, twin))

        @task("K" + t)
        def _():
            a, b, c = made["J" + t]
            arrived(a)
            ref = gh_rows(g, y_prev, 0, YR // 2)
            d = send(ref, ref, y_right)
            ref = gh_rows(g, y_prev, 0, YR)
            e = send(ref, ref, twin)
            arrived(b)
            ref = gh_rows(g, y_next, YR // 2, YR // 2)
            f = send(ref, ref, y_left)
            ref = gh_rows(g, y_next, 0, YR)
            i = send(ref, ref, twin)
            return d, f, c, e, i

        @task("L" + t)
        def _():
            d, f, c, e, i = made["K" + t]
            arrived(d, f)
            ref = gh_rows(g, y_far, 0, YR)
            return c, e, i, send(ref, ref, twin)

        @task("R" + t)
        def _():
            arrived(*made["L" + t])
            for name in ("I", "F", "J", "K", "L"):
                gone(*made[name + t])
            for name in ACTS:
                arrived(*made[name])
                gone(*made[name])

    for g in range(GROUPS):
        summed(g)

    def block_of(place):
        other, steps = ORDER[place]
        return lax.rem(z + other, 2) * 4 + lax.rem(x + steps, 4)

    def gradients(place):
        block = block_of(place)

        @pl.loop(0, 8)
        def _(i):
            pair = block * 2 + i // 4
            core = lax.rem(i // 2, 2)
            rows = at(lax.rem(i, 2) * 64, 64, 64)
            flat = at(place * B + i * 64, 64, 64)
            gate = act[0, pair, core, rows].astype(F32)
            up = act[1, pair, core, rows].astype(F32)
            grad = gh[flat].astype(F32)
            sig = jax.nn.sigmoid(gate)
            value = gate * sig
            act[0, pair, core, rows] = (value * up).astype(BF16)
            act[1, pair, core, rows] = (grad * up * sig * (1.0 + gate * (1.0 - sig))).astype(BF16)
            gh[flat] = (grad * value).astype(BF16)

    def input_terms(place, half=None):
        loaded(5)
        loaded(6)
        block = block_of(place)
        if half is None:
            grad_gate = act[1, pl.ds(block * 2, 2)].reshape(B, B)
            grad_up = gh[pl.ds(place * B, B)]
        else:
            grad_gate = act[1, block * 2 + half].reshape(B // 2, B)
            grad_up = gh[pl.ds(place * B + half * (B // 2), B // 2)]
        gate_term = lax.dot_general(grad_gate, wg_ref[...], NT, preferred_element_type=F32)
        return gate_term + lax.dot_general(grad_up, wu_ref[...], NT, preferred_element_type=F32)

    def send_halves(n, to):
        return tuple(send(x_out.at[n, rows], x_in.at[n, rows], to) for _, _, rows in halves)

    def out(name, n, where, to):
        @task("u" + name)
        def _():
            gradients(AT[where])
            x_out[n] = input_terms(AT[where]).astype(BF16)
            return send_halves(n, to)

    def ring(name, n, where, to, onward, source, m):
        @task("v" + name)
        def _():
            gradients(AT[where])

        for half, t, rows in halves:
            def one(half=half, t=t, rows=rows):
                @task("u" + name + t)
                def _():
                    total = input_terms(AT[where], half)
                    if t == onward:
                        arrived(made[source + t][0])
                        total = total + x_in[m, rows].astype(F32)
                    x_out[n, rows] = total.astype(BF16)
                    return (send(x_out.at[n, rows], x_in.at[n, rows], to),)
            one()

    if X_RING:
        ring("01", 0, (0, 1), x_right, "a", "u02", 5)
        ring("03", 1, (0, 3), x_left, "b", "u02", 5)
    else:
        out("01", 0, (0, 1), x_right)
        out("03", 1, (0, 3), x_left)
    if FAR_BY_X:
        ring("11", 3, (1, 1), x_right, "a", "u12", 2)
        ring("13", 4, (1, 3), x_left, "b", "u12", 2)
    else:
        out("11", 3, (1, 1), x_right)
        out("13", 4, (1, 3), x_left)

    @task("v12")
    def _():
        gradients(AT[1, 2])

    @task("v02")
    def _():
        gradients(AT[0, 2])

    @task("u00")
    def _():
        gradients(AT[0, 0])
        acc[0] = input_terms(AT[0, 0])

    @task("u10")
    def _():
        gradients(AT[1, 0])
        acc[1] = input_terms(AT[1, 0])

    def rest(half, t, rows):
        @task("u02" + t)
        def _():
            total = input_terms(AT[0, 2], half)
            if not FAR_BY_X:
                arrived(*made["u12" + t])
                total = total + x_in[2, rows].astype(F32)
            x_out[5, rows] = total.astype(BF16)
            to = (x_right if t == "a" else x_left) if X_RING else x_far
            return (send(x_out.at[5, rows], x_in.at[5, rows], to),)

        @task("u12" + t)
        def _():
            x_out[2, rows] = input_terms(AT[1, 2], half).astype(BF16)
            to = (x_right if t == "a" else x_left) if FAR_BY_X else z_pair
            return (send(x_out.at[2, rows], x_in.at[2, rows], to),)

        def sums_of(*names):
            for name in names:
                if name in made:
                    arrived(made[name][half])
                else:
                    arrived(*made[name + t])

        @task("s1" + t)
        def _():
            sums_of("u11", "u13")
            total = acc[1, rows] + x_in[3, rows].astype(F32) + x_in[4, rows].astype(F32)
            x_out[6, rows] = total.astype(BF16)
            return (send(x_out.at[6, rows], x_in.at[6, rows], z_pair),)

        @task("s0" + t)
        def _():
            sums_of("u01", "u03", "s1")
            total = acc[0, rows]
            if not X_RING:
                sums_of("u02")
                total = total + x_in[5, rows].astype(F32)
            for n in (0, 1, 6):
                total = total + x_in[n, rows].astype(F32)
            ig_ref[rows] = total.astype(BF16)
            return save(0, rows)

    for half, t, rows in halves:
        rest(half, t, rows)

    def weight_grads(places, which, out_ref, last):
        scale = (8 * B) ** -0.5
        total = None
        for place in places:
            block = block_of(place)
            if which == 0:
                left = act[0, pl.ds(block * 2, 2)].reshape(B, B)
                right = go[place]
            else:
                left = inp[place]
                if which == 1:
                    right = act[1, pl.ds(block * 2, 2)].reshape(B, B)
                else:
                    right = gh[pl.ds(place * B, B)]
            term = lax.dot_general(left, right, TN, preferred_element_type=F32)
            total = term if total is None else total + term
        if last:
            out_ref[...] = ((total + held[which]) * scale).astype(BF16)
        else:
            held[which] = total

    def weights(name, which, out_ref):
        @task(name + "0")
        def _():
            if which:
                for n in INS[:4]:
                    arrived(*made[n])
            weight_grads((0, 1, 2, 3), which, out_ref, False)

        @task(name + "1")
        def _():
            if which:
                for n in INS:
                    arrived(*made[n])
            weight_grads((4, 5, 6, 7), which, out_ref, True)
            save((3, 1, 2)[which])

    weights("d", 0, dg_ref)
    weights("g", 1, gg_ref)
    weights("w", 2, ug_ref)

    for name in SCHEDULE:
        tasks[name]()
    arrived(*range(len(copies)))
    gone(*range(len(copies)))
    for copy in saves:
        copy.wait()


def handed_on(*refs):
    held, sems = refs[8:]
    ins = [pltpu.make_async_copy(refs[n], held.at[n], sems.at[n]) for n in range(4)]
    outs = [pltpu.make_async_copy(held.at[n], refs[4 + n], sems.at[4 + n]) for n in range(4)]
    for move in ins:
        move.start()
    for n in range(4):
        ins[n].wait()
        outs[n].start()
    for move in outs:
        move.wait()


def per_device(*args):
    hbm = pl.BlockSpec(memory_space=pl.ANY)
    block = jax.ShapeDtypeStruct((B, B), BF16)
    made = pl.pallas_call(
        kernel,
        name="slab_backward",
        out_shape=(block,) * 4,
        in_specs=[hbm] * 7,
        out_specs=(hbm,) * 4,
        scratch_shapes=[
            pltpu.VMEM((3, B, B), BF16),
            pltpu.VMEM((4, B, B), BF16),
            pltpu.VMEM((8, B, B), BF16),
            pltpu.VMEM((8, B, B), BF16),
            pltpu.VMEM((2, 16, 2, ROWS, B), BF16),
            pltpu.VMEM((8 * B, B), BF16),
            pltpu.VMEM((GROUPS, HALF, B), F32),
            pltpu.VMEM((GROUPS, HALF, B), F32),
            pltpu.VMEM((GROUPS, HALF, B), F32),
            pltpu.VMEM((GROUPS, 3, YR, B), Y_TYPE),
            pltpu.VMEM((GROUPS, 3, YR, B), Y_TYPE),
            pltpu.VMEM((GROUPS, YR, B), F32),
            pltpu.VMEM((GROUPS, 3, HR, B), H_TYPE),
            pltpu.VMEM((GROUPS, 3, HR, B), H_TYPE),
            pltpu.VMEM((7, B, B), BF16),
            pltpu.VMEM((7, B, B), BF16),
            pltpu.VMEM((2, B, B), F32),
            pltpu.VMEM((3, B, B), F32),
            pltpu.SemaphoreType.DMA((200,)),
            pltpu.SemaphoreType.DMA((200,)),
            pltpu.SemaphoreType.DMA((12,)),
        ],
        compiler_params=pltpu.CompilerParams(
            collective_id=0, has_side_effects=True, vmem_limit_bytes=60 * 1024 * 1024
        ),
        cost_estimate=pl.CostEstimate(flops=12 * 4096 * B * B, bytes_accessed=12 * B * B, transcendentals=4096 * B),
    )(*args)
    return tuple(pl.pallas_call(
        handed_on,
        name="hand_on",
        out_shape=(block,) * 4,
        in_specs=[hbm] * 4,
        out_specs=(hbm,) * 4,
        scratch_shapes=[pltpu.VMEM((4, B, B), BF16), pltpu.SemaphoreType.DMA((8,))],
        compiler_params=pltpu.CompilerParams(vmem_limit_bytes=60 * 1024 * 1024),
    )(*made))


def solution(mesh):
    placed = (
        P("col", "row"),
        P("col", "row"),
        P("row", "col"),
        P("row", "col"),
        P("row", "col"),
        P("row", "col"),
        P("col", "row"),
    )
    return jax.shard_map(
        per_device,
        mesh=mesh,
        in_specs=placed,
        out_specs=(P("col", "row"), P("row", "col"), P("row", "col"), P("col", "row")),
        check_vma=False,
    )
```

```python
import functools

import jax
import jax.numpy as jnp
from jax import lax
from jax.experimental import pallas as pl
from jax.experimental.pallas import tpu as pltpu
from jax.sharding import PartitionSpec as P

MESH = pl.DeviceIdType.MESH
F32, BF16 = jnp.float32, jnp.bfloat16
B = 512
ROWS = 128
ORDER = ((0, 1), (0, 3), (1, 1), (1, 3), (0, 2), (1, 2), (0, 0), (1, 0))
AT = {where: place for place, where in enumerate(ORDER)}
GROUPS = 4
HALF = 8 * B // GROUPS // 2
YR = HALF // 4
HR = YR // 4
X_RING, FAR_BY_X = False, False
SPLIT = False
Y_DIRECT = False
Y_TYPE, H_TYPE = BF16, BF16
RING_IN, RING_OUT = False, False
INS = ("in0a", "in0b", "in3a", "in3b", "in1a", "in1b", "in2a", "in2b", "in4a", "in4b")
ACTS = ("a0", "a1", "a2", "a3", "bp", "bn", "bf", "cp", "cn", "cf", "t0", "t1", "t2")
SCHEDULE = (
    "go1a", "a1", "go0a", "go3a", "a0", "go0b", "go1b", "a3", "go3b", "P3",
    "P0", "Y3", "Y0", "Z3", "in1a", "Z0", "P1", "bn", "go2b", "in1b",
    "a2", "go4a", "go4b", "go2a", "Y1", "bp", "Z1", "in0a", "H0", "bf",
    "P2", "H1", "t0", "in0b", "Y2", "H3", "in3a", "I1", "cn", "I3",
    "Z2", "I0", "F3", "F1", "J1", "H2", "cp", "in2a", "cf", "F0",
    "t1", "in2b", "K1", "I2", "in3b", "J0", "in4a", "L1", "in4b", "t2",
    "J3", "F2", "K0", "J2", "R1", "u13", "u11", "L0", "K2", "R0",
    "u01", "K3", "L2", "R2", "v12", "u12a", "L3", "u03", "R3", "u10",
    "u12b", "u00", "v02", "w0", "s1a", "u02a", "w1", "u02b", "s1b", "d0",
    "g0", "g1", "d1", "s0a", "s0b",
)
NT = (((1,), (1,)), ((), ()))
TN = (((0,), (0,)), ((), ()))


def kernel(
    go_hbm, in_hbm, gate_hbm, up_hbm, wg_hbm, wu_hbm, wd_hbm,
    ig_hbm, gg_hbm, ug_hbm, dg_hbm,
    weights_in, results, go, inp, act, gh, part, own, core_in,
    y_out, y_in, h_sum, h_out, h_in, x_out, x_in, acc, held,
    send_sem, recv_sem, local_sem,
):
    row, col = lax.axis_index("row"), lax.axis_index("col")
    k, h, y = lax.rem(row, 2), lax.rem(row // 2, 4), row // 8
    x, z = lax.rem(col, 4), col // 4

    def row_of(y_, h_, k_):
        return (y_ * 4 + h_) * 2 + k_

    x_right, x_left, x_far = ((row, z * 4 + lax.rem(x + d, 4)) for d in (1, 3, 2))
    z_pair = (row, (1 - z) * 4 + x)
    y_next, y_prev, y_far = (lax.rem(y + d, 4) for d in (1, 3, 2))
    y_right, y_left, y_over = ((row_of(v, h, k), col) for v in (y_next, y_prev, y_far))
    h_next, h_prev, h_far = (lax.rem(h + d, 4) for d in (1, 3, 2))
    h_right, h_left, h_over = ((row_of(y, v, k), col) for v in (h_next, h_prev, h_far))
    twin = (row_of(y, h, 1 - k), col)
    friends = (x_right, x_left, z_pair, y_right, y_left, h_right, h_left, h_over, twin) + ((y_over,) if Y_DIRECT else ()) + (() if X_RING else (x_far,))

    mine = y * 4 + h
    loads = [
        pltpu.make_async_copy(src, dst, local_sem.at[n])
        for n, (src, dst) in enumerate((
            (go_hbm, go.at[AT[0, 0]]),
            (gate_hbm, act.at[0, mine, k]),
            (up_hbm, act.at[1, mine, k]),
            (wd_hbm, weights_in.at[2]),
            (in_hbm, inp.at[AT[0, 0]]),
            (wg_hbm, weights_in.at[0]),
            (wu_hbm, weights_in.at[1]),
        ))
    ]
    for load in loads:
        load.start()
    wg_ref, wu_ref, wd_ref = (weights_in.at[n] for n in range(3))
    ig_ref, gg_ref, ug_ref, dg_ref = (results.at[n] for n in range(4))

    barrier = pltpu.get_barrier_semaphore()
    for friend in friends:
        pl.semaphore_signal(barrier, inc=1, device_id=friend, device_id_type=MESH)
    pl.semaphore_wait(barrier, len(friends))

    for load in loads[:3]:
        load.wait()
    copies = []
    made = {}
    tasks = {}

    def send(src, dst, to):
        n = len(copies)
        copy = pltpu.make_async_remote_copy(
            src_ref=src, dst_ref=dst, send_sem=send_sem.at[n], recv_sem=recv_sem.at[n],
            device_id=to, device_id_type=MESH,
        )
        copy.start()
        copies.append([copy, False, False])
        return n

    waited = [True] * 3 + [False] * 4

    def loaded(n):
        if not waited[n]:
            loads[n].wait()
            waited[n] = True

    def arrived(*ns):
        for n in ns:
            if not copies[n][2]:
                copies[n][0].wait_recv()
                copies[n][2] = True

    def gone(*ns):
        for n in ns:
            if not copies[n][1]:
                copies[n][0].wait_send()
                copies[n][1] = True

    def task(name):
        def add(run):
            def step():
                made[name] = run()
            tasks[name] = step
            return run
        return add

    def at(start, n, step):
        return pl.ds(pl.multiple_of(start, step), n)

    first, second = pl.ds(0, B // 2), pl.ds(B // 2, B // 2)

    saves = []

    def save(n, rows=slice(None)):
        copy = pltpu.make_async_copy(
            results.at[n, rows], (ig_hbm, gg_hbm, ug_hbm, dg_hbm)[n].at[rows], local_sem.at[len(loads) + len(saves)]
        )
        copy.start()
        saves.append(copy)

    halves = ((0, "a", first), (1, "b", second))

    def gather(name, load, buf):
        mine = buf.at[AT[0, 0]]
        paired = buf.at[AT[1, 0]]

        def one(half, t, rows):
            part_of = rows if SPLIT else pl.ds(0, B)

            def both_ways(src, plane):
                return (
                    send(src, buf.at[AT[plane, 3], part_of], x_right),
                    send(src, buf.at[AT[plane, 1], part_of], x_left),
                )

            def far(plane):
                if half == 0:
                    return (send(buf.at[AT[plane, 3], rows], buf.at[AT[plane, 2], rows], x_right),)
                return (send(buf.at[AT[plane, 1], rows], buf.at[AT[plane, 2], rows], x_left),)

            @task(name + "0" + t)
            def _():
                loaded(load)
                if half == 1 and not SPLIT:
                    return made[name + "0a"]
                return both_ways(mine.at[part_of], 0)

            @task(name + "1" + t)
            def _():
                loaded(load)
                if half == 1 and not SPLIT:
                    return made[name + "1a"]
                return (send(mine.at[part_of], buf.at[AT[1, 0], part_of], z_pair),)

            @task(name + "2" + t)
            def _():
                arrived(made[name + "0" + t][half])
                return far(0)

            @task(name + "3" + t)
            def _():
                arrived(*made[name + "1" + t])
                if half == 1 and not SPLIT:
                    return made[name + "3a"]
                return both_ways(paired.at[part_of], 1)

            @task(name + "4" + t)
            def _():
                arrived(made[name + "3" + t][half])
                return far(1)

        for half, t, rows in halves:
            one(half, t, rows)

    gather("go", 0, go)
    gather("in", 4, inp)

    @task("a0")
    def _():
        ref = act.at[:, mine, k]
        return send(ref, ref, h_right), send(ref, ref, h_left)

    def act_to_y(h_):
        ref = act.at[:, y * 4 + h_, k]
        return send(ref, ref, y_right), send(ref, ref, y_left)

    def act_on_y(h_):
        ref = act.at[0, y_prev * 4 + h_, k]
        n = send(ref, ref, y_right)
        ref = act.at[1, y_next * 4 + h_, k]
        return n, send(ref, ref, y_left)

    @task("a1")
    def _():
        return act_to_y(h)

    @task("a2")
    def _():
        arrived(*made["a0"])
        ref = act.at[0, y * 4 + h_prev, k]
        n = send(ref, ref, h_right)
        ref = act.at[1, y * 4 + h_next, k]
        return n, send(ref, ref, h_left)

    @task("a3")
    def _():
        arrived(*made["a1"])
        return act_on_y(h)

    for name, h_, source in (("p", h_prev, "a0"), ("n", h_next, "a0"), ("f", h_far, "a2")):
        def pair(name=name, h_=h_, source=source):
            @task("b" + name)
            def _():
                arrived(*made[source])
                return act_to_y(h_)

            @task("c" + name)
            def _():
                arrived(*made["b" + name])
                return act_on_y(h_)
        pair()

    def act_twin(y_):
        ref = act.at[:, at(y_ * 4, 4, 4), k]
        return send(ref, ref, twin)

    @task("t0")
    def _():
        arrived(*made["a0"], *made["a2"])
        return (act_twin(y),)

    @task("t1")
    def _():
        arrived(*made["a1"], *made["bp"], *made["bn"], *made["bf"])
        return act_twin(y_prev), act_twin(y_next)

    @task("t2")
    def _():
        arrived(*made["a3"], *made["cp"], *made["cn"], *made["cf"])
        return (act_twin(y_far),)

    needs = (("go0a", "go0b"), ("go3a", "go3b"), ("go2a", "go2b", "go4a", "go4b"), ("go1a", "go1b"))

    def product(g, half, to):
        to[g] = lax.dot_general(go[g * 2 + half], wd_ref[...], NT, preferred_element_type=F32)

    def pair_sum(g, v, lo, n):
        rows = at(v * YR + lo, n, 64)
        return own[g, rows] + core_in[g, rows]

    lo, hi = pl.ds(0, YR // 2), pl.ds(YR // 2, YR // 2)

    def gh_rows(g, y_, start, n):
        return gh.at[at(g * 2 * HALF + k * HALF + y_ * YR + start, n, 16)]

    def summed(g):
        t = str(g)

        @task("P" + t)
        def _():
            for name in needs[g]:
                arrived(*made[name])
            loaded(3)
            product(g, 1 - k, part)
            n = send(part.at[g], core_in.at[g], twin)
            product(g, k, own)
            return (n,)

        @task("Y" + t)
        def _():
            arrived(*made["P" + t])
            y_out[g, 0] = pair_sum(g, y_far, 0, YR).astype(Y_TYPE)
            if Y_DIRECT:
                a = send(y_out.at[g, 0], y_in.at[g, 2], y_over)
                y_out[g, 1] = pair_sum(g, y_next, 0, YR).astype(Y_TYPE)
                b = send(y_out.at[g, 1], y_in.at[g, 0], y_right)
                y_out[g, 2] = pair_sum(g, y_prev, 0, YR).astype(Y_TYPE)
                return a, b, send(y_out.at[g, 2], y_in.at[g, 1], y_left)
            a = send(y_out.at[g, 0, lo], y_in.at[g, 2, lo], y_right)
            b = send(y_out.at[g, 0, hi], y_in.at[g, 2, hi], y_left)
            y_out[g, 1, hi] = pair_sum(g, y_next, YR // 2, YR // 2).astype(Y_TYPE)
            c = send(y_out.at[g, 1, hi], y_in.at[g, 0, hi], y_right)
            y_out[g, 2, lo] = pair_sum(g, y_prev, 0, YR // 2).astype(Y_TYPE)
            d = send(y_out.at[g, 2, lo], y_in.at[g, 1, lo], y_left)
            return a, b, c, d

        @task("Z" + t)
        def _():
            h_sum[g] = pair_sum(g, y, 0, YR)
            if Y_DIRECT:
                return made["Y" + t]
            a, b, c, d = made["Y" + t]
            arrived(a)
            y_out[g, 1, lo] = (pair_sum(g, y_next, 0, YR // 2) + y_in[g, 2, lo].astype(F32)).astype(Y_TYPE)
            e = send(y_out.at[g, 1, lo], y_in.at[g, 0, lo], y_right)
            arrived(b)
            y_out[g, 2, hi] = (pair_sum(g, y_prev, YR // 2, YR // 2) + y_in[g, 2, hi].astype(F32)).astype(Y_TYPE)
            f = send(y_out.at[g, 2, hi], y_in.at[g, 1, hi], y_left)
            return c, d, e, f

        @task("H" + t)
        def _():
            arrived(*made["Z" + t])
            total = h_sum[g] + y_in[g, 0].astype(F32) + y_in[g, 1].astype(F32)
            h_sum[g] = total + y_in[g, 2].astype(F32) if Y_DIRECT else total

            def piece(n, v):
                h_out[g, n] = h_sum[g, at(v * HR, HR, HR)].astype(H_TYPE)
                return h_out.at[g, n]

            return (
                send(piece(0, h_far), h_in.at[g, 2], h_over),
                send(piece(1, h_next), h_in.at[g, 0], h_right),
                send(piece(2, h_prev), h_in.at[g, 1], h_left),
            )

        @task("I" + t)
        def _():
            arrived(*made["H" + t])
            total = h_sum[g, at(h * HR, HR, HR)]
            for n in range(3):
                total = total + h_in[g, n].astype(F32)
            ref = gh_rows(g, y, h * HR, HR)
            ref[...] = total.astype(BF16)
            tos = (h_right, h_left) if RING_OUT else (h_over, h_right, h_left)
            return tuple(send(ref, ref, to) for to in tos)

        @task("F" + t)
        def _():
            if not RING_OUT:
                return made["I" + t]
            a, b = made["I" + t]
            arrived(a)
            ref = gh_rows(g, y, h_prev * HR, HR // 2)
            c = send(ref, ref, h_right)
            arrived(b)
            ref = gh_rows(g, y, h_next * HR + HR // 2, HR // 2)
            return a, b, c, send(ref, ref, h_left)

        @task("J" + t)
        def _():
            arrived(*made["F" + t])
            ref = gh_rows(g, y, 0, YR)
            return tuple(send(ref, ref, to) for to in (y_right, y_left, twin))

        @task("K" + t)
        def _():
            a, b, c = made["J" + t]
            arrived(a)
            ref = gh_rows(g, y_prev, 0, YR // 2)
            d = send(ref, ref, y_right)
            ref = gh_rows(g, y_prev, 0, YR)
            e = send(ref, ref, twin)
            arrived(b)
            ref = gh_rows(g, y_next, YR // 2, YR // 2)
            f = send(ref, ref, y_left)
            ref = gh_rows(g, y_next, 0, YR)
            i = send(ref, ref, twin)
            return d, f, c, e, i

        @task("L" + t)
        def _():
            d, f, c, e, i = made["K" + t]
            arrived(d, f)
            ref = gh_rows(g, y_far, 0, YR)
            return c, e, i, send(ref, ref, twin)

        @task("R" + t)
        def _():
            arrived(*made["L" + t])
            for name in ("I", "F", "J", "K", "L"):
                gone(*made[name + t])
            for name in ACTS:
                arrived(*made[name])
                gone(*made[name])

    for g in range(GROUPS):
        summed(g)

    def block_of(place):
        other, steps = ORDER[place]
        return lax.rem(z + other, 2) * 4 + lax.rem(x + steps, 4)

    def gradients(place):
        block = block_of(place)

        @pl.loop(0, 8)
        def _(i):
            pair = block * 2 + i // 4
            core = lax.rem(i // 2, 2)
            rows = at(lax.rem(i, 2) * 64, 64, 64)
            flat = at(place * B + i * 64, 64, 64)
            gate = act[0, pair, core, rows].astype(F32)
            up = act[1, pair, core, rows].astype(F32)
            grad = gh[flat].astype(F32)
            sig = jax.nn.sigmoid(gate)
            value = gate * sig
            act[0, pair, core, rows] = (value * up).astype(BF16)
            act[1, pair, core, rows] = (grad * up * sig * (1.0 + gate * (1.0 - sig))).astype(BF16)
            gh[flat] = (grad * value).astype(BF16)

    def input_terms(place, half=None):
        loaded(5)
        loaded(6)
        block = block_of(place)
        if half is None:
            grad_gate = act[1, pl.ds(block * 2, 2)].reshape(B, B)
            grad_up = gh[pl.ds(place * B, B)]
        else:
            grad_gate = act[1, block * 2 + half].reshape(B // 2, B)
            grad_up = gh[pl.ds(place * B + half * (B // 2), B // 2)]
        gate_term = lax.dot_general(grad_gate, wg_ref[...], NT, preferred_element_type=F32)
        return gate_term + lax.dot_general(grad_up, wu_ref[...], NT, preferred_element_type=F32)

    def send_halves(n, to):
        return tuple(send(x_out.at[n, rows], x_in.at[n, rows], to) for _, _, rows in halves)

    def out(name, n, where, to):
        @task("u" + name)
        def _():
            gradients(AT[where])
            x_out[n] = input_terms(AT[where]).astype(BF16)
            return send_halves(n, to)

    def ring(name, n, where, to, onward, source, m):
        @task("v" + name)
        def _():
            gradients(AT[where])

        for half, t, rows in halves:
            def one(half=half, t=t, rows=rows):
                @task("u" + name + t)
                def _():
                    total = input_terms(AT[where], half)
                    if t == onward:
                        arrived(made[source + t][0])
                        total = total + x_in[m, rows].astype(F32)
                    x_out[n, rows] = total.astype(BF16)
                    return (send(x_out.at[n, rows], x_in.at[n, rows], to),)
            one()

    if X_RING:
        ring("01", 0, (0, 1), x_right, "a", "u02", 5)
        ring("03", 1, (0, 3), x_left, "b", "u02", 5)
    else:
        out("01", 0, (0, 1), x_right)
        out("03", 1, (0, 3), x_left)
    if FAR_BY_X:
        ring("11", 3, (1, 1), x_right, "a", "u12", 2)
        ring("13", 4, (1, 3), x_left, "b", "u12", 2)
    else:
        out("11", 3, (1, 1), x_right)
        out("13", 4, (1, 3), x_left)

    @task("v12")
    def _():
        gradients(AT[1, 2])

    @task("v02")
    def _():
        gradients(AT[0, 2])

    @task("u00")
    def _():
        gradients(AT[0, 0])
        acc[0] = input_terms(AT[0, 0])

    @task("u10")
    def _():
        gradients(AT[1, 0])
        acc[1] = input_terms(AT[1, 0])

    def rest(half, t, rows):
        @task("u02" + t)
        def _():
            total = input_terms(AT[0, 2], half)
            if not FAR_BY_X:
                arrived(*made["u12" + t])
                total = total + x_in[2, rows].astype(F32)
            x_out[5, rows] = total.astype(BF16)
            to = (x_right if t == "a" else x_left) if X_RING else x_far
            return (send(x_out.at[5, rows], x_in.at[5, rows], to),)

        @task("u12" + t)
        def _():
            x_out[2, rows] = input_terms(AT[1, 2], half).astype(BF16)
            to = (x_right if t == "a" else x_left) if FAR_BY_X else z_pair
            return (send(x_out.at[2, rows], x_in.at[2, rows], to),)

        def sums_of(*names):
            for name in names:
                if name in made:
                    arrived(made[name][half])
                else:
                    arrived(*made[name + t])

        @task("s1" + t)
        def _():
            sums_of("u11", "u13")
            total = acc[1, rows] + x_in[3, rows].astype(F32) + x_in[4, rows].astype(F32)
            x_out[6, rows] = total.astype(BF16)
            return (send(x_out.at[6, rows], x_in.at[6, rows], z_pair),)

        @task("s0" + t)
        def _():
            sums_of("u01", "u03", "s1")
            total = acc[0, rows]
            if not X_RING:
                sums_of("u02")
                total = total + x_in[5, rows].astype(F32)
            for n in (0, 1, 6):
                total = total + x_in[n, rows].astype(F32)
            ig_ref[rows] = total.astype(BF16)
            return save(0, rows)

    for half, t, rows in halves:
        rest(half, t, rows)

    def weight_grads(places, which, out_ref, last):
        scale = (8 * B) ** -0.5
        total = None
        for place in places:
            block = block_of(place)
            if which == 0:
                left = act[0, pl.ds(block * 2, 2)].reshape(B, B)
                right = go[place]
            else:
                left = inp[place]
                if which == 1:
                    right = act[1, pl.ds(block * 2, 2)].reshape(B, B)
                else:
                    right = gh[pl.ds(place * B, B)]
            term = lax.dot_general(left, right, TN, preferred_element_type=F32)
            total = term if total is None else total + term
        if last:
            out_ref[...] = ((total + held[which]) * scale).astype(BF16)
        else:
            held[which] = total

    def weights(name, which, out_ref):
        @task(name + "0")
        def _():
            if which:
                for n in INS[:4]:
                    arrived(*made[n])
            weight_grads((0, 1, 2, 3), which, out_ref, False)

        @task(name + "1")
        def _():
            if which:
                for n in INS:
                    arrived(*made[n])
            weight_grads((4, 5, 6, 7), which, out_ref, True)
            save((3, 1, 2)[which])

    weights("d", 0, dg_ref)
    weights("g", 1, gg_ref)
    weights("w", 2, ug_ref)

    for name in SCHEDULE:
        tasks[name]()
    arrived(*range(len(copies)))
    gone(*range(len(copies)))
    for copy in saves:
        copy.wait()


def handed_on(*refs):
    held, sems = refs[8:]
    ins = [pltpu.make_async_copy(refs[n], held.at[n], sems.at[n]) for n in range(4)]
    outs = [pltpu.make_async_copy(held.at[n], refs[4 + n], sems.at[4 + n]) for n in range(4)]
    for move in ins:
        move.start()
    for n in range(4):
        ins[n].wait()
        outs[n].start()
    for move in outs:
        move.wait()


def per_device(*args):
    hbm = pl.BlockSpec(memory_space=pl.ANY)
    block = jax.ShapeDtypeStruct((B, B), BF16)
    made = pl.pallas_call(
        kernel,
        name="slab_backward",
        out_shape=(block,) * 4,
        in_specs=[hbm] * 7,
        out_specs=(hbm,) * 4,
        scratch_shapes=[
            pltpu.VMEM((3, B, B), BF16),
            pltpu.VMEM((4, B, B), BF16),
            pltpu.VMEM((8, B, B), BF16),
            pltpu.VMEM((8, B, B), BF16),
            pltpu.VMEM((2, 16, 2, ROWS, B), BF16),
            pltpu.VMEM((8 * B, B), BF16),
            pltpu.VMEM((GROUPS, HALF, B), F32),
            pltpu.VMEM((GROUPS, HALF, B), F32),
            pltpu.VMEM((GROUPS, HALF, B), F32),
            pltpu.VMEM((GROUPS, 3, YR, B), Y_TYPE),
            pltpu.VMEM((GROUPS, 3, YR, B), Y_TYPE),
            pltpu.VMEM((GROUPS, YR, B), F32),
            pltpu.VMEM((GROUPS, 3, HR, B), H_TYPE),
            pltpu.VMEM((GROUPS, 3, HR, B), H_TYPE),
            pltpu.VMEM((7, B, B), BF16),
            pltpu.VMEM((7, B, B), BF16),
            pltpu.VMEM((2, B, B), F32),
            pltpu.VMEM((3, B, B), F32),
            pltpu.SemaphoreType.DMA((200,)),
            pltpu.SemaphoreType.DMA((200,)),
            pltpu.SemaphoreType.DMA((12,)),
        ],
        compiler_params=pltpu.CompilerParams(
            collective_id=0, has_side_effects=True, vmem_limit_bytes=60 * 1024 * 1024
        ),
        cost_estimate=pl.CostEstimate(flops=12 * 4096 * B * B, bytes_accessed=12 * B * B, transcendentals=4096 * B),
    )(*args)
    return tuple(pl.pallas_call(
        handed_on,
        name="hand_on",
        out_shape=(block,) * 4,
        in_specs=[hbm] * 4,
        out_specs=(hbm,) * 4,
        scratch_shapes=[pltpu.VMEM((4, B, B), BF16), pltpu.SemaphoreType.DMA((8,))],
        compiler_params=pltpu.CompilerParams(vmem_limit_bytes=60 * 1024 * 1024),
    )(*made))


def solution(mesh):
    placed = (
        P("col", "row"),
        P("col", "row"),
        P("row", "col"),
        P("row", "col"),
        P("row", "col"),
        P("row", "col"),
        P("col", "row"),
    )
    return jax.shard_map(
        per_device,
        mesh=mesh,
        in_specs=placed,
        out_specs=(P("col", "row"), P("row", "col"), P("row", "col"), P("col", "row")),
        check_vma=False,
    )
```

```python
import functools

import jax
import jax.numpy as jnp
from jax import lax
from jax.experimental import pallas as pl
from jax.experimental.pallas import tpu as pltpu
from jax.sharding import PartitionSpec as P

MESH = pl.DeviceIdType.MESH
F32, BF16 = jnp.float32, jnp.bfloat16
B = 512
ROWS = 128
ORDER = ((0, 1), (0, 3), (1, 1), (1, 3), (0, 2), (1, 2), (0, 0), (1, 0))
AT = {where: place for place, where in enumerate(ORDER)}
GROUPS = 4
HALF = 8 * B // GROUPS // 2
YR = HALF // 4
HR = YR // 4
X_RING, FAR_BY_X = False, False
SPLIT = False
Y_DIRECT = False
Y_TYPE, H_TYPE = BF16, BF16
RING_IN, RING_OUT = False, False
INS = ("in0a", "in0b", "in3a", "in3b", "in1a", "in1b", "in2a", "in2b", "in4a", "in4b")
ACTS = ("a0", "a1", "a2", "a3", "bp", "bn", "bf", "cp", "cn", "cf", "t0", "t1", "t2")
SCHEDULE = (
    "go1a", "a1", "go0a", "go3a", "go1b", "a0", "a3", "go0b", "P0", "P3",
    "Y0", "go3b", "Y3", "Z0", "go2a", "in1a", "go2b", "Z3", "go4a", "go4b",
    "P1", "bp", "a2", "Y1", "in1b", "bn", "Z1", "in0a", "P2", "H0",
    "Y2", "H1", "bf", "in0b", "in3a", "I0", "cn", "Z2", "I1", "cp",
    "H2", "in2a", "F1", "J1", "t0", "t1", "in3b", "H3", "cf", "in4b",
    "F0", "I2", "in2b", "F2", "K1", "in4a", "J0", "t2", "L1", "I3",
    "J2", "R1", "u13", "K0", "u11", "K2", "L0", "R0", "u03", "L2",
    "F3", "J3", "R2", "v12", "u12a", "u01", "K3", "u12b", "w0", "g0",
    "L3", "v02", "R3", "u10", "s1a", "u02a", "s1b", "u02b", "u00", "g1",
    "d0", "d1", "w1", "s0a", "s0b",
)
NT = (((1,), (1,)), ((), ()))
TN = (((0,), (0,)), ((), ()))


def kernel(
    go_hbm, in_hbm, gate_hbm, up_hbm, wg_hbm, wu_hbm, wd_hbm,
    ig_hbm, gg_hbm, ug_hbm, dg_hbm,
    weights_in, results, go, inp, act, gh, part, own, core_in,
    y_out, y_in, h_sum, h_out, h_in, x_out, x_in, acc, held,
    send_sem, recv_sem, local_sem,
):
    row, col = lax.axis_index("row"), lax.axis_index("col")
    k, h, y = lax.rem(row, 2), lax.rem(row // 2, 4), row // 8
    x, z = lax.rem(col, 4), col // 4

    def row_of(y_, h_, k_):
        return (y_ * 4 + h_) * 2 + k_

    x_right, x_left, x_far = ((row, z * 4 + lax.rem(x + d, 4)) for d in (1, 3, 2))
    z_pair = (row, (1 - z) * 4 + x)
    y_next, y_prev, y_far = (lax.rem(y + d, 4) for d in (1, 3, 2))
    y_right, y_left, y_over = ((row_of(v, h, k), col) for v in (y_next, y_prev, y_far))
    h_next, h_prev, h_far = (lax.rem(h + d, 4) for d in (1, 3, 2))
    h_right, h_left, h_over = ((row_of(y, v, k), col) for v in (h_next, h_prev, h_far))
    twin = (row_of(y, h, 1 - k), col)
    friends = (x_right, x_left, z_pair, y_right, y_left, h_right, h_left, h_over, twin) + ((y_over,) if Y_DIRECT else ()) + (() if X_RING else (x_far,))

    mine = y * 4 + h
    loads = [
        pltpu.make_async_copy(src, dst, local_sem.at[n])
        for n, (src, dst) in enumerate((
            (go_hbm, go.at[AT[0, 0]]),
            (gate_hbm, act.at[0, mine, k]),
            (up_hbm, act.at[1, mine, k]),
            (wd_hbm, weights_in.at[2]),
            (in_hbm, inp.at[AT[0, 0]]),
            (wg_hbm, weights_in.at[0]),
            (wu_hbm, weights_in.at[1]),
        ))
    ]
    for load in loads:
        load.start()
    wg_ref, wu_ref, wd_ref = (weights_in.at[n] for n in range(3))
    ig_ref, gg_ref, ug_ref, dg_ref = (results.at[n] for n in range(4))

    barrier = pltpu.get_barrier_semaphore()
    for friend in friends:
        pl.semaphore_signal(barrier, inc=1, device_id=friend, device_id_type=MESH)
    pl.semaphore_wait(barrier, len(friends))

    for load in loads[:3]:
        load.wait()
    copies = []
    made = {}
    tasks = {}

    def send(src, dst, to):
        n = len(copies)
        copy = pltpu.make_async_remote_copy(
            src_ref=src, dst_ref=dst, send_sem=send_sem.at[n], recv_sem=recv_sem.at[n],
            device_id=to, device_id_type=MESH,
        )
        copy.start()
        copies.append([copy, False, False])
        return n

    waited = [True] * 3 + [False] * 4

    def loaded(n):
        if not waited[n]:
            loads[n].wait()
            waited[n] = True

    def arrived(*ns):
        for n in ns:
            if not copies[n][2]:
                copies[n][0].wait_recv()
                copies[n][2] = True

    def gone(*ns):
        for n in ns:
            if not copies[n][1]:
                copies[n][0].wait_send()
                copies[n][1] = True

    def task(name):
        def add(run):
            def step():
                made[name] = run()
            tasks[name] = step
            return run
        return add

    def at(start, n, step):
        return pl.ds(pl.multiple_of(start, step), n)

    first, second = pl.ds(0, B // 2), pl.ds(B // 2, B // 2)

    saves = []

    def save(n, rows=slice(None)):
        copy = pltpu.make_async_copy(
            results.at[n, rows], (ig_hbm, gg_hbm, ug_hbm, dg_hbm)[n].at[rows], local_sem.at[len(loads) + len(saves)]
        )
        copy.start()
        saves.append(copy)

    halves = ((0, "a", first), (1, "b", second))

    def gather(name, load, buf):
        mine = buf.at[AT[0, 0]]
        paired = buf.at[AT[1, 0]]

        def one(half, t, rows):
            part_of = rows if SPLIT else pl.ds(0, B)

            def both_ways(src, plane):
                return (
                    send(src, buf.at[AT[plane, 3], part_of], x_right),
                    send(src, buf.at[AT[plane, 1], part_of], x_left),
                )

            def far(plane):
                if half == 0:
                    return (send(buf.at[AT[plane, 3], rows], buf.at[AT[plane, 2], rows], x_right),)
                return (send(buf.at[AT[plane, 1], rows], buf.at[AT[plane, 2], rows], x_left),)

            @task(name + "0" + t)
            def _():
                loaded(load)
                if half == 1 and not SPLIT:
                    return made[name + "0a"]
                return both_ways(mine.at[part_of], 0)

            @task(name + "1" + t)
            def _():
                loaded(load)
                if half == 1 and not SPLIT:
                    return made[name + "1a"]
                return (send(mine.at[part_of], buf.at[AT[1, 0], part_of], z_pair),)

            @task(name + "2" + t)
            def _():
                arrived(made[name + "0" + t][half])
                return far(0)

            @task(name + "3" + t)
            def _():
                arrived(*made[name + "1" + t])
                if half == 1 and not SPLIT:
                    return made[name + "3a"]
                return both_ways(paired.at[part_of], 1)

            @task(name + "4" + t)
            def _():
                arrived(made[name + "3" + t][half])
                return far(1)

        for half, t, rows in halves:
            one(half, t, rows)

    gather("go", 0, go)
    gather("in", 4, inp)

    @task("a0")
    def _():
        ref = act.at[:, mine, k]
        return send(ref, ref, h_right), send(ref, ref, h_left)

    def act_to_y(h_):
        ref = act.at[:, y * 4 + h_, k]
        return send(ref, ref, y_right), send(ref, ref, y_left)

    def act_on_y(h_):
        ref = act.at[0, y_prev * 4 + h_, k]
        n = send(ref, ref, y_right)
        ref = act.at[1, y_next * 4 + h_, k]
        return n, send(ref, ref, y_left)

    @task("a1")
    def _():
        return act_to_y(h)

    @task("a2")
    def _():
        arrived(*made["a0"])
        ref = act.at[0, y * 4 + h_prev, k]
        n = send(ref, ref, h_right)
        ref = act.at[1, y * 4 + h_next, k]
        return n, send(ref, ref, h_left)

    @task("a3")
    def _():
        arrived(*made["a1"])
        return act_on_y(h)

    for name, h_, source in (("p", h_prev, "a0"), ("n", h_next, "a0"), ("f", h_far, "a2")):
        def pair(name=name, h_=h_, source=source):
            @task("b" + name)
            def _():
                arrived(*made[source])
                return act_to_y(h_)

            @task("c" + name)
            def _():
                arrived(*made["b" + name])
                return act_on_y(h_)
        pair()

    def act_twin(y_):
        ref = act.at[:, at(y_ * 4, 4, 4), k]
        return send(ref, ref, twin)

    @task("t0")
    def _():
        arrived(*made["a0"], *made["a2"])
        return (act_twin(y),)

    @task("t1")
    def _():
        arrived(*made["a1"], *made["bp"], *made["bn"], *made["bf"])
        return act_twin(y_prev), act_twin(y_next)

    @task("t2")
    def _():
        arrived(*made["a3"], *made["cp"], *made["cn"], *made["cf"])
        return (act_twin(y_far),)

    needs = (("go0a", "go0b"), ("go3a", "go3b"), ("go2a", "go2b", "go4a", "go4b"), ("go1a", "go1b"))

    def product(g, half, to):
        to[g] = lax.dot_general(go[g * 2 + half], wd_ref[...], NT, preferred_element_type=F32)

    def pair_sum(g, v, lo, n):
        rows = at(v * YR + lo, n, 64)
        return own[g, rows] + core_in[g, rows]

    lo, hi = pl.ds(0, YR // 2), pl.ds(YR // 2, YR // 2)

    def gh_rows(g, y_, start, n):
        return gh.at[at(g * 2 * HALF + k * HALF + y_ * YR + start, n, 16)]

    def summed(g):
        t = str(g)

        @task("P" + t)
        def _():
            for name in needs[g]:
                arrived(*made[name])
            loaded(3)
            product(g, 1 - k, part)
            n = send(part.at[g], core_in.at[g], twin)
            product(g, k, own)
            return (n,)

        @task("Y" + t)
        def _():
            arrived(*made["P" + t])
            y_out[g, 0] = pair_sum(g, y_far, 0, YR).astype(Y_TYPE)
            if Y_DIRECT:
                a = send(y_out.at[g, 0], y_in.at[g, 2], y_over)
                y_out[g, 1] = pair_sum(g, y_next, 0, YR).astype(Y_TYPE)
                b = send(y_out.at[g, 1], y_in.at[g, 0], y_right)
                y_out[g, 2] = pair_sum(g, y_prev, 0, YR).astype(Y_TYPE)
                return a, b, send(y_out.at[g, 2], y_in.at[g, 1], y_left)
            a = send(y_out.at[g, 0, lo], y_in.at[g, 2, lo], y_right)
            b = send(y_out.at[g, 0, hi], y_in.at[g, 2, hi], y_left)
            y_out[g, 1, hi] = pair_sum(g, y_next, YR // 2, YR // 2).astype(Y_TYPE)
            c = send(y_out.at[g, 1, hi], y_in.at[g, 0, hi], y_right)
            y_out[g, 2, lo] = pair_sum(g, y_prev, 0, YR // 2).astype(Y_TYPE)
            d = send(y_out.at[g, 2, lo], y_in.at[g, 1, lo], y_left)
            return a, b, c, d

        @task("Z" + t)
        def _():
            h_sum[g] = pair_sum(g, y, 0, YR)
            if Y_DIRECT:
                return made["Y" + t]
            a, b, c, d = made["Y" + t]
            arrived(a)
            y_out[g, 1, lo] = (pair_sum(g, y_next, 0, YR // 2) + y_in[g, 2, lo].astype(F32)).astype(Y_TYPE)
            e = send(y_out.at[g, 1, lo], y_in.at[g, 0, lo], y_right)
            arrived(b)
            y_out[g, 2, hi] = (pair_sum(g, y_prev, YR // 2, YR // 2) + y_in[g, 2, hi].astype(F32)).astype(Y_TYPE)
            f = send(y_out.at[g, 2, hi], y_in.at[g, 1, hi], y_left)
            return c, d, e, f

        @task("H" + t)
        def _():
            arrived(*made["Z" + t])
            total = h_sum[g] + y_in[g, 0].astype(F32) + y_in[g, 1].astype(F32)
            h_sum[g] = total + y_in[g, 2].astype(F32) if Y_DIRECT else total

            def piece(n, v):
                h_out[g, n] = h_sum[g, at(v * HR, HR, HR)].astype(H_TYPE)
                return h_out.at[g, n]

            return (
                send(piece(0, h_far), h_in.at[g, 2], h_over),
                send(piece(1, h_next), h_in.at[g, 0], h_right),
                send(piece(2, h_prev), h_in.at[g, 1], h_left),
            )

        @task("I" + t)
        def _():
            arrived(*made["H" + t])
            total = h_sum[g, at(h * HR, HR, HR)]
            for n in range(3):
                total = total + h_in[g, n].astype(F32)
            ref = gh_rows(g, y, h * HR, HR)
            ref[...] = total.astype(BF16)
            tos = (h_right, h_left) if RING_OUT else (h_over, h_right, h_left)
            return tuple(send(ref, ref, to) for to in tos)

        @task("F" + t)
        def _():
            if not RING_OUT:
                return made["I" + t]
            a, b = made["I" + t]
            arrived(a)
            ref = gh_rows(g, y, h_prev * HR, HR // 2)
            c = send(ref, ref, h_right)
            arrived(b)
            ref = gh_rows(g, y, h_next * HR + HR // 2, HR // 2)
            return a, b, c, send(ref, ref, h_left)

        @task("J" + t)
        def _():
            arrived(*made["F" + t])
            ref = gh_rows(g, y, 0, YR)
            return tuple(send(ref, ref, to) for to in (y_right, y_left, twin))

        @task("K" + t)
        def _():
            a, b, c = made["J" + t]
            arrived(a)
            ref = gh_rows(g, y_prev, 0, YR // 2)
            d = send(ref, ref, y_right)
            ref = gh_rows(g, y_prev, 0, YR)
            e = send(ref, ref, twin)
            arrived(b)
            ref = gh_rows(g, y_next, YR // 2, YR // 2)
            f = send(ref, ref, y_left)
            ref = gh_rows(g, y_next, 0, YR)
            i = send(ref, ref, twin)
            return d, f, c, e, i

        @task("L" + t)
        def _():
            d, f, c, e, i = made["K" + t]
            arrived(d, f)
            ref = gh_rows(g, y_far, 0, YR)
            return c, e, i, send(ref, ref, twin)

        @task("R" + t)
        def _():
            arrived(*made["L" + t])
            for name in ("I", "F", "J", "K", "L"):
                gone(*made[name + t])
            for name in ACTS:
                arrived(*made[name])
                gone(*made[name])

    for g in range(GROUPS):
        summed(g)

    def block_of(place):
        other, steps = ORDER[place]
        return lax.rem(z + other, 2) * 4 + lax.rem(x + steps, 4)

    def gradients(place):
        block = block_of(place)

        @pl.loop(0, 8)
        def _(i):
            pair = block * 2 + i // 4
            core = lax.rem(i // 2, 2)
            rows = at(lax.rem(i, 2) * 64, 64, 64)
            flat = at(place * B + i * 64, 64, 64)
            gate = act[0, pair, core, rows].astype(F32)
            up = act[1, pair, core, rows].astype(F32)
            grad = gh[flat].astype(F32)
            sig = jax.nn.sigmoid(gate)
            value = gate * sig
            act[0, pair, core, rows] = (value * up).astype(BF16)
            act[1, pair, core, rows] = (grad * up * sig * (1.0 + gate * (1.0 - sig))).astype(BF16)
            gh[flat] = (grad * value).astype(BF16)

    def input_terms(place, half=None):
        loaded(5)
        loaded(6)
        block = block_of(place)
        if half is None:
            grad_gate = act[1, pl.ds(block * 2, 2)].reshape(B, B)
            grad_up = gh[pl.ds(place * B, B)]
        else:
            grad_gate = act[1, block * 2 + half].reshape(B // 2, B)
            grad_up = gh[pl.ds(place * B + half * (B // 2), B // 2)]
        gate_term = lax.dot_general(grad_gate, wg_ref[...], NT, preferred_element_type=F32)
        return gate_term + lax.dot_general(grad_up, wu_ref[...], NT, preferred_element_type=F32)

    def send_halves(n, to):
        return tuple(send(x_out.at[n, rows], x_in.at[n, rows], to) for _, _, rows in halves)

    def out(name, n, where, to):
        @task("u" + name)
        def _():
            gradients(AT[where])
            x_out[n] = input_terms(AT[where]).astype(BF16)
            return send_halves(n, to)

    def ring(name, n, where, to, onward, source, m):
        @task("v" + name)
        def _():
            gradients(AT[where])

        for half, t, rows in halves:
            def one(half=half, t=t, rows=rows):
                @task("u" + name + t)
                def _():
                    total = input_terms(AT[where], half)
                    if t == onward:
                        arrived(made[source + t][0])
                        total = total + x_in[m, rows].astype(F32)
                    x_out[n, rows] = total.astype(BF16)
                    return (send(x_out.at[n, rows], x_in.at[n, rows], to),)
            one()

    if X_RING:
        ring("01", 0, (0, 1), x_right, "a", "u02", 5)
        ring("03", 1, (0, 3), x_left, "b", "u02", 5)
    else:
        out("01", 0, (0, 1), x_right)
        out("03", 1, (0, 3), x_left)
    if FAR_BY_X:
        ring("11", 3, (1, 1), x_right, "a", "u12", 2)
        ring("13", 4, (1, 3), x_left, "b", "u12", 2)
    else:
        out("11", 3, (1, 1), x_right)
        out("13", 4, (1, 3), x_left)

    @task("v12")
    def _():
        gradients(AT[1, 2])

    @task("v02")
    def _():
        gradients(AT[0, 2])

    @task("u00")
    def _():
        gradients(AT[0, 0])
        acc[0] = input_terms(AT[0, 0])

    @task("u10")
    def _():
        gradients(AT[1, 0])
        acc[1] = input_terms(AT[1, 0])

    def rest(half, t, rows):
        @task("u02" + t)
        def _():
            total = input_terms(AT[0, 2], half)
            if not FAR_BY_X:
                arrived(*made["u12" + t])
                total = total + x_in[2, rows].astype(F32)
            x_out[5, rows] = total.astype(BF16)
            to = (x_right if t == "a" else x_left) if X_RING else x_far
            return (send(x_out.at[5, rows], x_in.at[5, rows], to),)

        @task("u12" + t)
        def _():
            x_out[2, rows] = input_terms(AT[1, 2], half).astype(BF16)
            to = (x_right if t == "a" else x_left) if FAR_BY_X else z_pair
            return (send(x_out.at[2, rows], x_in.at[2, rows], to),)

        def sums_of(*names):
            for name in names:
                if name in made:
                    arrived(made[name][half])
                else:
                    arrived(*made[name + t])

        @task("s1" + t)
        def _():
            sums_of("u11", "u13")
            total = acc[1, rows] + x_in[3, rows].astype(F32) + x_in[4, rows].astype(F32)
            x_out[6, rows] = total.astype(BF16)
            return (send(x_out.at[6, rows], x_in.at[6, rows], z_pair),)

        @task("s0" + t)
        def _():
            sums_of("u01", "u03", "s1")
            total = acc[0, rows]
            if not X_RING:
                sums_of("u02")
                total = total + x_in[5, rows].astype(F32)
            for n in (0, 1, 6):
                total = total + x_in[n, rows].astype(F32)
            ig_ref[rows] = total.astype(BF16)
            return save(0, rows)

    for half, t, rows in halves:
        rest(half, t, rows)

    def weight_grads(places, which, out_ref, last):
        scale = (8 * B) ** -0.5
        total = None
        for place in places:
            block = block_of(place)
            if which == 0:
                left = act[0, pl.ds(block * 2, 2)].reshape(B, B)
                right = go[place]
            else:
                left = inp[place]
                if which == 1:
                    right = act[1, pl.ds(block * 2, 2)].reshape(B, B)
                else:
                    right = gh[pl.ds(place * B, B)]
            term = lax.dot_general(left, right, TN, preferred_element_type=F32)
            total = term if total is None else total + term
        if last:
            out_ref[...] = ((total + held[which]) * scale).astype(BF16)
        else:
            held[which] = total

    def weights(name, which, out_ref):
        @task(name + "0")
        def _():
            if which:
                for n in INS[:4]:
                    arrived(*made[n])
            weight_grads((0, 1, 2, 3), which, out_ref, False)

        @task(name + "1")
        def _():
            if which:
                for n in INS:
                    arrived(*made[n])
            weight_grads((4, 5, 6, 7), which, out_ref, True)
            save((3, 1, 2)[which])

    weights("d", 0, dg_ref)
    weights("g", 1, gg_ref)
    weights("w", 2, ug_ref)

    for name in SCHEDULE:
        tasks[name]()
    arrived(*range(len(copies)))
    gone(*range(len(copies)))
    for copy in saves:
        copy.wait()


def handed_on(*refs):
    held, sems = refs[8:]
    ins = [pltpu.make_async_copy(refs[n], held.at[n], sems.at[n]) for n in range(4)]
    outs = [pltpu.make_async_copy(held.at[n], refs[4 + n], sems.at[4 + n]) for n in range(4)]
    for move in ins:
        move.start()
    for n in range(4):
        ins[n].wait()
        outs[n].start()
    for move in outs:
        move.wait()


def per_device(*args):
    hbm = pl.BlockSpec(memory_space=pl.ANY)
    block = jax.ShapeDtypeStruct((B, B), BF16)
    made = pl.pallas_call(
        kernel,
        name="slab_backward",
        out_shape=(block,) * 4,
        in_specs=[hbm] * 7,
        out_specs=(hbm,) * 4,
        scratch_shapes=[
            pltpu.VMEM((3, B, B), BF16),
            pltpu.VMEM((4, B, B), BF16),
            pltpu.VMEM((8, B, B), BF16),
            pltpu.VMEM((8, B, B), BF16),
            pltpu.VMEM((2, 16, 2, ROWS, B), BF16),
            pltpu.VMEM((8 * B, B), BF16),
            pltpu.VMEM((GROUPS, HALF, B), F32),
            pltpu.VMEM((GROUPS, HALF, B), F32),
            pltpu.VMEM((GROUPS, HALF, B), F32),
            pltpu.VMEM((GROUPS, 3, YR, B), Y_TYPE),
            pltpu.VMEM((GROUPS, 3, YR, B), Y_TYPE),
            pltpu.VMEM((GROUPS, YR, B), F32),
            pltpu.VMEM((GROUPS, 3, HR, B), H_TYPE),
            pltpu.VMEM((GROUPS, 3, HR, B), H_TYPE),
            pltpu.VMEM((7, B, B), BF16),
            pltpu.VMEM((7, B, B), BF16),
            pltpu.VMEM((2, B, B), F32),
            pltpu.VMEM((3, B, B), F32),
            pltpu.SemaphoreType.DMA((200,)),
            pltpu.SemaphoreType.DMA((200,)),
            pltpu.SemaphoreType.DMA((12,)),
        ],
        compiler_params=pltpu.CompilerParams(
            collective_id=0, has_side_effects=True, vmem_limit_bytes=60 * 1024 * 1024
        ),
        cost_estimate=pl.CostEstimate(flops=12 * 4096 * B * B, bytes_accessed=12 * B * B, transcendentals=4096 * B),
    )(*args)
    return tuple(pl.pallas_call(
        handed_on,
        name="hand_on",
        out_shape=(block,) * 4,
        in_specs=[hbm] * 4,
        out_specs=(hbm,) * 4,
        scratch_shapes=[pltpu.VMEM((4, B, B), BF16), pltpu.SemaphoreType.DMA((8,))],
        compiler_params=pltpu.CompilerParams(vmem_limit_bytes=60 * 1024 * 1024),
    )(*made))


def solution(mesh):
    placed = (
        P("col", "row"),
        P("col", "row"),
        P("row", "col"),
        P("row", "col"),
        P("row", "col"),
        P("row", "col"),
        P("col", "row"),
    )
    return jax.shard_map(
        per_device,
        mesh=mesh,
        in_specs=placed,
        out_specs=(P("col", "row"), P("row", "col"), P("row", "col"), P("col", "row")),
        check_vma=False,
    )
```
